32 devices in a mesh: parts: 2 (over y), clu: 4 (over z), sub: 2 (over x), rep: 2 (over core).
Axes of the slice: x: 2, y: 2, z: 4, core: 2. Of those that a mesh axis runs over, the one named last changes fastest.
Arguments:
- panel_field: bfloat16 [16, 512, 256], P(('parts', 'clu'), 'sub'), parts along dimension 0, may hold values from -6 to 6
- near_row: int32 [416], P(('parts', 'clu', 'rep')), parts along dimension 0, may hold values from 0 to 1
- near_col: int32 [416], P(('parts', 'clu', 'rep')), parts along dimension 0, may hold values from 0 to 7, as said below
- near_block: bfloat16 [416, 512, 512], P(('parts', 'clu', 'rep'), None, 'sub'), parts along dimension 0, may hold values from -0.0625 to 0.0625
- bases: bfloat16 [16, 512, 32], P(('parts', 'clu'), 'sub'), parts along dimension 0, may hold values from -0.25 to 0.25
- far_row: int32 [512], P(('parts', 'clu', 'rep')), parts along dimension 0, may hold values from 0 to 1
- far_col: int32 [512], P(('parts', 'clu', 'rep')), parts along dimension 0, may hold values from 0 to 7, as said below
- coupling: float32 [512, 32, 32], P(('parts', 'clu', 'rep')), parts along dimension 0, may hold values from -1 to 1
Outputs:
- product: float32 [16, 512, 256], P(('parts', 'clu'), 'sub'), parts along dimension 0
The draws below stay inside these ranges and needn't reach their ends.
There are 2 independent parts, one for each index of `parts`. The reference program is written for one: setup_inputs(seed, part) draws one part's arguments, and reference() takes and returns one part's arrays. A program takes and returns all parts, laid end to end along the dimension named above; each array names one. Nothing has to cross between parts.
Inputs may be any that keep to these rules, and one draw needn't show every extreme that they name: Among the 26 near pairs of one device (aligned blocks of near_col) at most 13 have column clusters c with c // 2 equal to one index of clu, and in each such block some index of clu is named by exactly 13 of them. Among the 32 far pairs of one device (aligned blocks of far_col) at most 16 have column clusters c with c // 2 equal to one index of clu, and in each such block some index of clu is named by exactly 16 of them.
All inputs are finite; a program needn't handle non-finite values.
Results may differ from the reference program's by a relative error of at most 0.0015.
Values may be sent and summed in bfloat16 or wider, within the bound.
No kernel may reach another device: no remote copies, remote signals or barrier semaphores. Data moves between devices by JAX's collectives and lax.ppermute only.
A program may use at most 128 MiB of HBM per device.

```python
import jax
import jax.numpy as jnp
from jax import lax

B = 512
R = 32
NRHS = 256
CL_DEV = 2
NEAR_DEV = 26
FAR_DEV = 32
NC = 8
NPAIRS = 208
NFARS = 256
CAP = 13
CAPF = 16
N_REP = 2


def owner_columns(subkey, count, limit, owners):
    first_key, second_key, third_key, fourth_key = jax.random.split(subkey, 4)
    forced = jax.random.randint(first_key, (), 0, owners).astype(jnp.int32)
    spare_slots = jax.random.permutation(second_key, (owners - 1) * limit)[:count - limit]
    others = (spare_slots // limit).astype(jnp.int32)
    others = others + (others >= forced).astype(jnp.int32)
    chosen = jnp.concatenate([jnp.full((limit,), forced, jnp.int32), others])
    chosen = jax.random.permutation(third_key, chosen)
    local_ids = jax.random.randint(fourth_key, (count,), 0, CL_DEV).astype(jnp.int32)
    return chosen * CL_DEV + local_ids


def draw_near_col(key, part):
    key = jax.random.fold_in(key, 11)
    owners = NC // CL_DEV
    group_keys = jax.random.split(key, NPAIRS // NEAR_DEV)
    columns = jax.vmap(lambda subkey: owner_columns(subkey, NEAR_DEV, CAP, owners))(group_keys)
    return columns.reshape(-1)


def draw_far_col(key, part):
    key = jax.random.fold_in(key, 12)
    owners = NC // CL_DEV
    group_keys = jax.random.split(key, NFARS // FAR_DEV)
    columns = jax.vmap(lambda subkey: owner_columns(subkey, FAR_DEV, CAPF, owners))(group_keys)
    return columns.reshape(-1)


def touch_ends(entries, own_key, least, largest):
    dims = entries.shape
    spot = [jax.random.randint(jax.random.fold_in(own_key, axis), (), 0, dims[axis]) for axis in range(len(dims))]
    entries = entries.at[tuple(spot)].set(least)
    longest = dims.index(max(dims))
    spot[longest] = (spot[longest] + 1) % dims[longest]
    return entries.at[tuple(spot)].set(largest)


def level_of(key, dims, pieces, least, largest):
    loudness = 1.0
    for dim, shards_of in pieces:
        draws = jax.random.uniform(jax.random.fold_in(jax.random.fold_in(key, 6), dim), (shards_of,), jnp.float32, least / len(pieces), largest / len(pieces))
        loudness = loudness * jnp.repeat(jnp.exp(draws), dims[dim] // shards_of).reshape((-1,) + (1,) * (len(dims) - 1 - dim))
    return loudness


def bell_draw(own_key, extent, scale, most, cuts=(), kind=jnp.bfloat16):
    array = jax.random.normal(own_key, extent, jnp.float32) * scale
    if len(cuts) > 0:
        array = level_of(own_key, extent, cuts, -0.22, 0.18) * array
    return jnp.clip(array, min=-most, max=most).astype(kind)


def setup_inputs(seed: int = 0, part: int = 0) -> dict:
    splits = jax.random.split(jax.random.key(seed), 9)
    own_keys = jax.random.split(jax.random.fold_in(splits[8], part), 9)
    return {
        "panel_field": bell_draw(own_keys[0], (NC, B, NRHS), 1.0, 6.0, ((0, 4), (1, 2))),
        "near_row": touch_ends(jax.random.randint(own_keys[1], (NPAIRS,), 0, CL_DEV), jax.random.fold_in(own_keys[1], 1), 0, CL_DEV - 1).astype(jnp.int32),
        "near_col": draw_near_col(jax.random.fold_in(jax.random.fold_in(splits[8], part), 71), part),
        "near_block": bell_draw(own_keys[3], (NPAIRS, B, B), (B * 16) ** -0.5, 0.0625, ((0, 8), (2, 2))),
        "bases": bell_draw(own_keys[4], (NC, B, R), B ** -0.5, 0.25, ((0, 4), (1, 2))),
        "far_row": touch_ends(jax.random.randint(own_keys[5], (NFARS,), 0, CL_DEV), jax.random.fold_in(own_keys[5], 1), 0, CL_DEV - 1).astype(jnp.int32),
        "far_col": draw_far_col(jax.random.fold_in(jax.random.fold_in(splits[8], part), 71), part),
        "coupling": bell_draw(own_keys[7], (NFARS, R, R), R ** -0.5, 1.0, ((0, 8),), jnp.float32),
    }


def reference(panel_field, near_row, near_col, near_block, bases, far_row, far_col, coupling):
    groups = NPAIRS // NEAR_DEV
    owner_base = (jnp.arange(groups, dtype=jnp.int32) // N_REP) * CL_DEV
    near_rows = near_row.reshape(groups, NEAR_DEV) + owner_base[:, None]
    near_cols = near_col.reshape(groups, NEAR_DEV)
    block_groups = near_block.reshape(groups, NEAR_DEV, B, B)
    field = panel_field.astype(jnp.float32)

    def near_step(group, result):
        row_ids = near_rows[group]
        col_ids = near_cols[group]
        block_set = block_groups[group].astype(jnp.float32)
        forward = jnp.einsum("pab,pbk->pak", block_set, field[col_ids])
        backward = jnp.einsum("pab,pak->pbk", block_set, field[row_ids]).astype(jnp.bfloat16)
        backward = lax.optimization_barrier(backward).astype(jnp.float32)
        return result.at[row_ids].add(forward).at[col_ids].add(backward)

    result = lax.fori_loop(0, groups, near_step, jnp.zeros((NC, B, NRHS), jnp.float32))
    basis_full = bases.astype(jnp.float32)
    projection = jnp.einsum("cbr,cbk->crk", basis_full, field)
    far_rows = (far_row.reshape(groups, FAR_DEV) + owner_base[:, None]).reshape(-1)
    row_terms = jnp.einsum("pab,pbk->pak", coupling, projection[far_col], precision=lax.Precision.HIGHEST)
    col_terms = jnp.einsum("pab,pak->pbk", coupling, projection[far_rows], precision=lax.Precision.HIGHEST)
    weights = jnp.zeros((NC, R, NRHS), jnp.float32).at[far_rows].add(row_terms).at[far_col].add(col_terms)
    far_field = jnp.einsum("cbr,crk->cbk", basis_full, weights, precision=lax.Precision.HIGHEST)
    return result + far_field
```

```python
import functools

import jax
import jax.numpy as jnp
from jax import lax
from jax.experimental import pallas as pl
from jax.experimental.pallas import tpu as pltpu
from jax.sharding import PartitionSpec as P

HIGHEST = lax.Precision.HIGHEST
LAST = (((1,), (1,)), ((), ()))
FIRST = (((0,), (0,)), ((), ()))
VMEM = pl.BlockSpec(memory_space=pltpu.VMEM)
SMEM = pl.BlockSpec(memory_space=pltpu.SMEM)
ANY = pl.BlockSpec(memory_space=pl.ANY)
ROOM = pltpu.CompilerParams(vmem_limit_bytes=48 * 1024 * 1024)


def pack_kernel(where, panel, bases, packed, mine):
    clusters, _, width = panel.shape
    for c in range(clusters):
        packed[c, :width, :] = panel[c].T
        packed[c, width:, :] = bases[c].T
    mine[0] = packed[where[2]]


def pack(where, panel, bases):
    clusters, panels, width = panel.shape
    rows = width + bases.shape[2]
    return pl.pallas_call(
        pack_kernel,
        out_shape=(
            jax.ShapeDtypeStruct((clusters, rows, panels), panel.dtype),
            jax.ShapeDtypeStruct((1, rows, panels), panel.dtype),
        ),
        in_specs=[SMEM, VMEM, VMEM],
        out_specs=(VMEM, VMEM),
        compiler_params=ROOM,
    )(where, panel, bases)


def sum_couplings(far_row, far_slot, coupling, table):
    table[...] = jnp.zeros_like(table)
    for f in range(coupling.shape[0]):
        at = (far_row[f], far_slot[f])
        table[at] = table[at] + coupling[f]


def coupling_matrix(table):
    clusters, slots = table.shape[:2]
    return jnp.concatenate(
        [jnp.concatenate([table[c, t] for t in range(slots)], axis=1) for c in range(clusters)],
        axis=0,
    )


def load_blocks(block, held, sems, group):
    copies = []
    for n in range(block.shape[0] // group):
        span = pl.ds(n * group, group)
        copies.append(pltpu.make_async_copy(block.at[span], held.at[span], sems.at[n]))
        copies[-1].start()
    return copies


def back_kernel(plan, split, *refs):
    n = len(plan)
    place, near_row, near_slot, far_row, far_slot, coupling, block = refs[:7]
    pieces = refs[7 : 7 + n]
    outs = refs[7 + n : 7 + n + (2 if split else 1)]
    full, table, held, sems, piece_sems = refs[7 + n + len(outs) : 12 + n + len(outs)]
    total = refs[12 + n + len(outs)] if split else outs[0]
    group = 2 if block.shape[0] % 2 == 0 else 1
    panels = block.shape[2]
    clusters, rows = full.shape[:2]
    rank = table.shape[2]
    width = rows - rank
    moves = []
    for k, count in enumerate(plan):
        for c in range(count):
            moves.append(
                pltpu.make_async_copy(
                    pieces[k].at[c],
                    full.at[
                        place[2 * k] + c,
                        :,
                        pl.ds(pl.multiple_of(place[2 * k + 1] * panels, panels), panels),
                    ],
                    piece_sems.at[len(moves)],
                )
            )
            moves[-1].start()
    copies = load_blocks(block, held, sems, group)
    total[:, :width, :] = jnp.zeros((total.shape[0], width, panels), jnp.float32)
    sum_couplings(far_row, far_slot, coupling, table)
    for move in moves:
        move.wait()
    projection = jnp.concatenate(
        [
            lax.dot_general(
                full[c, width:, :], full[c, :width, :], LAST, preferred_element_type=jnp.float32
            )
            for c in range(clusters)
        ],
        axis=0,
    )
    weights = lax.dot_general(
        coupling_matrix(table),
        projection,
        FIRST,
        precision=HIGHEST,
        preferred_element_type=jnp.float32,
    )
    for t in range(total.shape[0]):
        for i in range(width // panels):
            total[t, width + i * rank : width + (i + 1) * rank, :] = weights[
                t * rank : (t + 1) * rank, i * panels : (i + 1) * panels
            ]
    for q in range(block.shape[0]):
        if q % group == 0:
            copies[q // group].wait()
        product = jnp.dot(
            full[near_row[q], :width, :], held[q], preferred_element_type=jnp.float32
        )
        slot = near_slot[q]
        total[slot, :width, :] += product.astype(jnp.bfloat16).astype(jnp.float32)
    if split:
        half = total.shape[0] // 2
        outs[0][...] = total[:half]
        outs[1][...] = total[half:]


def back_sums(slots, split, pieces, near_row, near_slot, far_row, far_slot, coupling, block):
    plan = tuple(piece.shape[0] for piece, _, _ in pieces)
    place = jnp.stack([jnp.asarray(v, jnp.int32) for _, c, s in pieces for v in (c, s)])
    rows = pieces[0][0].shape[1]
    pairs, full_panels, panels = block.shape
    rank = coupling.shape[1]
    width = rows - rank
    tall = width + rank * (width // panels)
    count = slots // 2 if split else slots
    shape = jax.ShapeDtypeStruct((count, tall, panels), jnp.float32)
    scratch = [
        pltpu.VMEM((2, rows, full_panels), jnp.bfloat16),
        pltpu.VMEM((2, slots, rank, rank), jnp.float32),
        pltpu.VMEM(block.shape, block.dtype),
        pltpu.SemaphoreType.DMA((pairs,)),
        pltpu.SemaphoreType.DMA((sum(plan),)),
    ]
    if split:
        scratch.append(pltpu.VMEM((slots, tall, panels), jnp.float32))
    return pl.pallas_call(
        functools.partial(back_kernel, plan, split),
        out_shape=(shape,) * (2 if split else 1),
        in_specs=[SMEM] * 5 + [VMEM, ANY] + [ANY] * len(pieces),
        out_specs=(VMEM,) * (2 if split else 1),
        scratch_shapes=scratch,
        compiler_params=ROOM,
    )(
        place, near_row, near_slot, far_row, far_slot, coupling, block, *[p for p, _, _ in pieces]
    )


def forward_kernel(plan, *refs):
    n = len(plan)
    place, near_row, near_col, far_row, far_col, coupling, block = refs[:7]
    pieces = refs[7 : 7 + n]
    keep, give = refs[7 + n : 9 + n]
    full, table, held, total, sems, piece_sems = refs[9 + n :]
    group = 2 if block.shape[0] % 2 == 0 else 1
    slots, rows, panels = full.shape
    rank = table.shape[2]
    width = rows - rank
    full_panels = block.shape[1]
    moves = []
    for k, count in enumerate(plan):
        moves.append(
            pltpu.make_async_copy(
                pieces[k], full.at[pl.ds(place[2 + k], count)], piece_sems.at[k]
            )
        )
        moves[-1].start()
    copies = load_blocks(block, held, sems, group)
    total[...] = jnp.zeros_like(total)
    sum_couplings(far_row, far_col, coupling, table)
    for move in moves:
        move.wait()
    projection = jnp.concatenate(
        [
            lax.dot_general(
                full[t, width:, :], full[t, :width, :], LAST, preferred_element_type=jnp.float32
            )
            for t in range(slots)
        ],
        axis=0,
    )
    weights = jnp.dot(
        coupling_matrix(table), projection, precision=HIGHEST, preferred_element_type=jnp.float32
    )
    for q in range(block.shape[0]):
        if q % group == 0:
            copies[q // group].wait()
        product = lax.dot_general(
            held[q], full[near_col[q], :width, :], LAST, preferred_element_type=jnp.float32
        )
        row = near_row[q]
        total[row] += product
    mine = place[0]
    core = place[1]
    subs = full_panels // panels
    for out, at in ((keep, core), (give, 1 - core)):
        for step in range(1, subs):
            other = lax.rem(mine + step, subs)
            out[0, (step - 1) * panels : step * panels, :] = total[
                at, pl.ds(pl.multiple_of(other * panels, panels), panels), :
            ]
        first = (subs - 1) * panels
        out[0, first + rank :, :] = total[at, pl.ds(pl.multiple_of(mine * panels, panels), panels), :]
        for c in range(2):

            @pl.when(at == c)
            def _():
                out[0, first : first + rank, :] = weights[c * rank : (c + 1) * rank]


def forward_sums(sub, core, slots, pieces, near_row, near_col, far_row, far_col, coupling, block):
    plan = tuple(piece.shape[0] for piece, _ in pieces)
    place = jnp.stack([jnp.asarray(v, jnp.int32) for v in (sub, core, *[c for _, c in pieces])])
    rows = pieces[0][0].shape[1]
    pairs, full_panels, panels = block.shape
    rank = coupling.shape[1]
    width = rows - rank
    shape = jax.ShapeDtypeStruct((1, full_panels + rank, width), jnp.float32)
    return pl.pallas_call(
        functools.partial(forward_kernel, plan),
        out_shape=(shape, shape),
        in_specs=[SMEM] * 5 + [VMEM, ANY] + [ANY] * len(pieces),
        out_specs=(VMEM, VMEM),
        scratch_shapes=[
            pltpu.VMEM((slots, rows, panels), jnp.bfloat16),
            pltpu.VMEM((2, slots, rank, rank), jnp.float32),
            pltpu.VMEM(block.shape, block.dtype),
            pltpu.VMEM((2, full_panels, width), jnp.float32),
            pltpu.SemaphoreType.DMA((pairs,)),
            pltpu.SemaphoreType.DMA((len(pieces),)),
        ],
        compiler_params=ROOM,
    )(place, near_row, near_col, far_row, far_col, coupling, block, *[p for p, _ in pieces])


def finish_kernel(where, packed, both, single, near, far, result, back, weight):
    core = where[2]
    clusters, rows, panels = packed.shape
    width = near.shape[1]
    rank = rows - width
    back[...] = both[...].astype(jnp.float32)
    back[core] = back[core] + single[0]
    for c in range(clusters):
        for i in range(width // panels):
            weight[c, :, i * panels : (i + 1) * panels] = back[
                c, width + i * rank : width + (i + 1) * rank, :
            ]
    weight[core] = weight[core] + far[...]
    for c in range(clusters):
        result[c] = back[c, :width, :].T + lax.dot_general(
            packed[c, width:, :].astype(jnp.float32),
            weight[c],
            FIRST,
            precision=HIGHEST,
            preferred_element_type=jnp.float32,
        )
    result[core] = result[core] + near[...]


def finish(where, packed, both, single, near, far):
    clusters, _, panels = packed.shape
    return pl.pallas_call(
        finish_kernel,
        out_shape=jax.ShapeDtypeStruct((clusters,) + near.shape, jnp.float32),
        in_specs=[SMEM] + [VMEM] * 5,
        out_specs=VMEM,
        scratch_shapes=[
            pltpu.VMEM(both.shape, jnp.float32),
            pltpu.VMEM((clusters,) + far.shape, jnp.float32),
        ],
        compiler_params=ROOM,
    )(where, packed, both, single, near, far)


def swap(value, axis):
    return lax.ppermute(value, axis, [(0, 1), (1, 0)])


def shards_small(panel_field, near_row, near_col, near_block, bases, far_row, far_col, coupling):
    owner, sub, core = lax.axis_index("clu"), lax.axis_index("sub"), lax.axis_index("rep")
    where = jnp.stack([owner, sub, core]).astype(jnp.int32)
    panels = panel_field.shape[1]
    rank = bases.shape[2]
    packed, mine = pack(where, panel_field, bases)

    axes = ("clu", "sub", "rep")
    numbered = [(o, s, r) for o in range(4) for s in range(2) for r in range(2)]
    by_core = [
        (i, ((o ^ (1 + r)) * 2 + s) * 2 + r) for i, (o, s, r) in enumerate(numbered)
    ]
    opposite = [(o, o ^ 3) for o in range(4)]

    def spread(two, one):
        return lax.ppermute(two, axes, by_core), lax.ppermute(one, "clu", opposite)

    across = swap(mine, "sub")
    across_other = swap(across, "rep")
    first, second = spread(packed, mine)

    def slot_of(cluster):
        turn = (cluster // 2) ^ owner
        local = cluster % 2
        paired = (turn == 1) | (turn == 2)
        kept = jnp.where(paired, turn == 1 + core, local == core)
        within = jnp.where(paired, local, jnp.where(turn == 3, 2, 3))
        return jnp.where(kept, within, 4 + within).astype(jnp.int32)

    keep, give = back_sums(
        8,
        True,
        [(packed, 0, sub), (across, core, 1 - sub), (across_other, 1 - core, 1 - sub)],
        near_row,
        slot_of(near_col),
        far_row,
        slot_of(far_col),
        coupling,
        near_block,
    )
    taken = swap(give, "rep")
    to_two = (keep[:2] + taken[:2]).astype(jnp.bfloat16)
    to_one = (keep[2:3] + taken[2:3]).astype(jnp.bfloat16)
    own = keep[3:] + taken[3:]
    back_two, back_one = spread(to_two, to_one)

    first_other, second_other = swap(first, "rep"), swap(second, "rep")
    ahead, behind = forward_sums(
        sub,
        core,
        8,
        [
            (packed, 2 * owner),
            (first, 2 * (owner ^ (1 + core))),
            (first_other, 2 * (owner ^ (2 - core))),
            (second, 2 * (owner ^ 3) + core),
            (second_other, 2 * (owner ^ 3) + 1 - core),
        ],
        near_row,
        near_col,
        far_row,
        far_col,
        coupling,
        near_block,
    )
    behind_other = swap(behind, "rep")
    split = panels + rank
    to_sub = ahead[0, :split] + behind_other[0, :split]
    stays = ahead[0, split:] + behind_other[0, split:]
    from_sub = swap(to_sub, "sub")
    near = stays + from_sub[:panels]
    far = to_sub[panels:] + from_sub[panels:]
    single = own + back_one.astype(jnp.float32)
    result = finish(where, packed, back_two, single, near, far)
    return result + swap(result, "rep")


def shards_any(panel_field, near_row, near_col, near_block, bases, far_row, far_col, coupling):
    owner, sub, core = lax.axis_index("clu"), lax.axis_index("sub"), lax.axis_index("rep")
    owners, subs = lax.axis_size("clu"), lax.axis_size("sub")
    where = jnp.stack([owner, sub, core]).astype(jnp.int32)
    clusters, panels, _ = panel_field.shape
    rank = bases.shape[2]
    packed, _ = pack(where, panel_field, bases)
    around = lax.all_gather(packed, "sub", axis=0)
    gathered = lax.all_gather(packed, "clu", axis=0, tiled=True)
    slots = owners * clusters
    (back,) = back_sums(
        slots,
        False,
        [(around[s], 0, s) for s in range(subs)],
        near_row,
        near_col,
        far_row,
        far_col,
        coupling,
        near_block,
    )
    back = lax.psum(lax.psum_scatter(back, "clu", scatter_dimension=0, tiled=True), "rep")
    ahead, behind = forward_sums(
        sub, core, slots, [(gathered, 0)], near_row, near_col, far_row, far_col, coupling, near_block
    )
    total = (ahead + swap(behind, "rep"))[0]
    first = (subs - 1) * panels
    far = lax.psum(total[first : first + rank], "sub")
    near = total[first + rank :]
    for step in range(1, subs):
        near = near + lax.ppermute(
            total[(step - 1) * panels : step * panels],
            "sub",
            [(s, (s + step) % subs) for s in range(subs)],
        )
    single = lax.dynamic_slice_in_dim(back, core, 1, axis=0)
    result = finish(where, packed, jnp.zeros_like(back), single, near, far)
    return result + swap(result, "rep")


def shards(*arrays):
    sizes = tuple(lax.axis_size(axis) for axis in ("clu", "sub", "rep"))
    if sizes == (4, 2, 2):
        return shards_small(*arrays)
    return shards_any(*arrays)


def solution(mesh):
    placed = (
        P(("parts", "clu"), "sub", None),
        P(("parts", "clu", "rep")),
        P(("parts", "clu", "rep")),
        P(("parts", "clu", "rep"), None, "sub"),
        P(("parts", "clu"), "sub", None),
        P(("parts", "clu", "rep")),
        P(("parts", "clu", "rep")),
        P(("parts", "clu", "rep"), None, None),
    )
    return jax.shard_map(
        shards,
        mesh=mesh,
        in_specs=placed,
        out_specs=P(("parts", "clu"), "sub", None),
        check_vma=False,
    )
```

```python
import functools

import jax
import jax.numpy as jnp
from jax import lax
from jax.experimental import pallas as pl
from jax.experimental.pallas import tpu as pltpu
from jax.sharding import PartitionSpec as P

HIGHEST = lax.Precision.HIGHEST
LAST = (((1,), (1,)), ((), ()))
FIRST = (((0,), (0,)), ((), ()))
VMEM = pl.BlockSpec(memory_space=pltpu.VMEM)
SMEM = pl.BlockSpec(memory_space=pltpu.SMEM)
ANY = pl.BlockSpec(memory_space=pl.ANY)
ROOM = pltpu.CompilerParams(vmem_limit_bytes=32 * 1024 * 1024)


def cost(flops, moved):
    return pl.CostEstimate(flops=flops, bytes_accessed=moved, transcendentals=0)


COST1 = cost(0, 0)
COST2 = cost(0, 0)
COST3 = cost(1 << 30, 1 << 20)


def in_hbm(array):
    return pltpu.with_memory_space_constraint(array, pltpu.HBM)


PARTS = 3


def parts_of(block, held, sems):
    pairs = block.shape[0]
    cuts = [pairs * k // PARTS for k in range(PARTS + 1)]
    return [
        (
            range(a, b),
            pltpu.make_async_copy(block.at[pl.ds(a, b - a)], held.at[pl.ds(a, b - a)], sems.at[k]),
        )
        for k, (a, b) in enumerate(zip(cuts, cuts[1:]))
    ]


def load_kernel(block, held, sems):
    parts = parts_of(block, held, sems)
    for _, copy in parts:
        copy.start()
    for _, copy in parts:
        copy.wait()


def load(block):
    return pl.pallas_call(
        load_kernel,
        out_shape=jax.ShapeDtypeStruct(block.shape, block.dtype),
        in_specs=[ANY],
        out_specs=VMEM,
        scratch_shapes=[pltpu.SemaphoreType.DMA((PARTS,))],
        compiler_params=ROOM,
    )(in_hbm(block))


def pack_kernel(index, panel, bases, packed, mine, held, sems):
    clusters, _, width = panel.shape
    moves = []
    for c in range(clusters):
        moves.append(pltpu.make_async_copy(panel.at[c], held.at[c], sems.at[2 * c]))
        moves.append(
            pltpu.make_async_copy(bases.at[c], packed.at[c, pl.ds(width, bases.shape[1])], sems.at[2 * c + 1])
        )
    for move in moves:
        move.start()
    for c in range(clusters):
        moves[2 * c].wait()
        packed[c, :width, :] = held[c].T
    for c in range(clusters):
        moves[2 * c + 1].wait()
    mine[0] = packed[index[2]]


def pack(index, panel, bases):
    clusters, panels, width = panel.shape
    rows = width + bases.shape[1]
    return pl.pallas_call(
        pack_kernel,
        out_shape=(
            jax.ShapeDtypeStruct((clusters, rows, panels), panel.dtype),
            jax.ShapeDtypeStruct((1, rows, panels), panel.dtype),
        ),
        in_specs=[SMEM, ANY, ANY],
        out_specs=(VMEM, VMEM),
        scratch_shapes=[
            pltpu.VMEM(panel.shape, panel.dtype),
            pltpu.SemaphoreType.DMA((2 * clusters,)),
        ],
        compiler_params=ROOM,
    )(index, in_hbm(panel), in_hbm(bases))


def sum_couplings(row, slot, coupling, table):
    table[...] = jnp.zeros_like(table)
    for f in range(coupling.shape[0]):
        at = (row(f), slot(f))
        table[at] = table[at] + coupling[f]


def coupling_matrix(table):
    clusters, slots = table.shape[:2]
    return jnp.concatenate(
        [jnp.concatenate([table[c, t] for t in range(slots)], axis=1) for c in range(clusters)],
        axis=0,
    )


def each_pair(pairs, step):
    unroll = 13 if pairs % 13 == 0 else 1

    def several(n, carry):
        for k in range(unroll):
            step(n * unroll + k)
        return carry

    lax.fori_loop(0, pairs // unroll, several, 0)


def back_kernel(plan, slot_of, index, starts, coupling, block, *refs):
    n = len(plan)
    pieces = refs[:n]
    total, full, table, held, sems = refs[n:]
    near_row, near_col, far_row, far_col = starts
    parts = parts_of(block, held, sems)
    for _, copy in parts:
        copy.start()
    panels = block.shape[2]
    clusters, rows = full.shape[:2]
    rank = table.shape[2]
    width = rows - rank

    total[:, :width, :] = jnp.zeros((total.shape[0], width, panels), jnp.float32)
    sum_couplings(
        lambda f: index[far_row + f],
        lambda f: slot_of(index[far_col + f], index[0], index[2]),
        coupling,
        table,
    )
    for piece, where in zip(pieces, plan):
        first, sub = where(index[0], index[1], index[2])
        for c in range(piece.shape[0]):
            full[first + c, :, pl.ds(pl.multiple_of(sub * panels, panels), panels)] = piece[c]
    projection = jnp.concatenate(
        [
            lax.dot_general(
                full[c, width:, :], full[c, :width, :], LAST, preferred_element_type=jnp.float32
            )
            for c in range(clusters)
        ],
        axis=0,
    )
    weights = lax.dot_general(
        coupling_matrix(table),
        projection,
        FIRST,
        precision=HIGHEST,
        preferred_element_type=jnp.float32,
    )
    for t in range(total.shape[0]):
        for i in range(width // panels):
            total[t, width + i * rank : width + (i + 1) * rank, :] = weights[
                t * rank : (t + 1) * rank, i * panels : (i + 1) * panels
            ]

    def step(q):
        product = jnp.dot(
            full[index[near_row + q], :width, :], held[q], preferred_element_type=jnp.float32
        )
        slot = slot_of(index[near_col + q], index[0], index[2])
        total[slot, :width, :] += product.astype(jnp.bfloat16).astype(jnp.float32)

    for pairs, copy in parts:
        copy.wait()
        for q in pairs:
            step(q)


def back_sums(slots, slot_of, pieces, index, starts, coupling, block):
    rows = pieces[0][0].shape[1]
    pairs, full_panels, panels = block.shape
    rank = coupling.shape[1]
    width = rows - rank
    tall = width + rank * (width // panels)
    plan = tuple(where for _, where in pieces)

    def kernel(index, *refs):
        back_kernel(plan, slot_of, index, starts, *refs)

    return pl.pallas_call(
        kernel,
        out_shape=jax.ShapeDtypeStruct((slots, tall, panels), jnp.float32),
        in_specs=[SMEM, VMEM, ANY] + [VMEM] * len(pieces),
        out_specs=VMEM,
        scratch_shapes=[
            pltpu.VMEM((2, rows, full_panels), jnp.bfloat16),
            pltpu.VMEM((2, slots, rank, rank), jnp.float32),
            pltpu.VMEM(block.shape, block.dtype),
            pltpu.SemaphoreType.DMA((PARTS,)),
        ],
        compiler_params=ROOM,
        cost_estimate=COST1,
    )(index, coupling, in_hbm(block), *[p for p, _ in pieces])


def forward_rows(turns, index, starts, block, full, total):
    near_row, near_col, _, _ = starts
    rows, panels = total.shape[1] // len(turns), block.shape[2]
    subs = block.shape[1] // panels
    total[...] = jnp.zeros_like(total)

    def step(q):
        field = full[index[near_col + q], : total.shape[2], :]
        row = index[near_row + q]
        for k, turn in enumerate(turns):
            at = lax.rem(index[1] + turn, subs)
            product = lax.dot_general(
                block[q, pl.ds(pl.multiple_of(at * panels, panels), panels), :],
                field,
                LAST,
                preferred_element_type=jnp.float32,
            )
            total[row, k * rows : (k + 1) * rows, :] += product

    each_pair(block.shape[0], step)


def forward_kernel(plan, turns, index, starts, coupling, block, *refs):
    n = len(plan)
    pieces = refs[:n]
    keep, give, full, table, total = refs[n:]
    _, _, far_row, far_col = starts
    slots, rows, _ = full.shape
    rank = table.shape[2]
    width = rows - rank
    sum_couplings(lambda f: index[far_row + f], lambda f: index[far_col + f], coupling, table)
    for piece, where in zip(pieces, plan):
        first = where(index[0], index[1], index[2])
        for c in range(piece.shape[0]):
            full[first + c] = piece[c]
    projection = jnp.concatenate(
        [
            lax.dot_general(
                full[t, width:, :], full[t, :width, :], LAST, preferred_element_type=jnp.float32
            )
            for t in range(slots)
        ],
        axis=0,
    )
    weights = jnp.dot(
        coupling_matrix(table), projection, precision=HIGHEST, preferred_element_type=jnp.float32
    )
    forward_rows(turns, index, starts, block, full, total)
    core, tall = index[2], total.shape[1]
    keep[:tall, :] = total[core]
    keep[tall:, :] = weights
    give[:tall, :] = total[1 - core]
    give[tall:, :] = weights


def forward_far(slots, pieces, index, starts, coupling, block):
    rows = pieces[0][0].shape[1]
    pairs, full_panels, panels = block.shape
    rank = coupling.shape[1]
    width = rows - rank
    plan = tuple(where for _, where in pieces)
    turns = tuple(range(1, full_panels // panels))
    tall = panels * len(turns)
    shape = jax.ShapeDtypeStruct((tall + 2 * rank, width), jnp.float32)

    def kernel(index, *refs):
        forward_kernel(plan, turns, index, starts, *refs)

    return pl.pallas_call(
        kernel,
        out_shape=(shape, shape, jax.ShapeDtypeStruct((slots, rows, panels), jnp.bfloat16)),
        in_specs=[SMEM] + [VMEM] * (2 + len(pieces)),
        out_specs=(VMEM, VMEM, VMEM),
        scratch_shapes=[
            pltpu.VMEM((2, slots, rank, rank), jnp.float32),
            pltpu.VMEM((2, tall, width), jnp.float32),
        ],
        compiler_params=ROOM,
        cost_estimate=COST2,
    )(index, coupling, block, *[p for p, _ in pieces])


def merge_kernel(index, keep, taken, payload, far):
    rank = far.shape[1]
    panels = keep.shape[0] - 2 * rank
    core = index[2]
    for c in range(2):
        rows = slice(panels + c * rank, panels + (c + 1) * rank)
        far[c] = keep[rows, :] + taken[rows, :]
    weights = far[core]
    high = weights.astype(payload.dtype)
    payload[:panels, :] = (keep[:panels] + taken[:panels]).astype(payload.dtype)
    payload[panels : panels + rank, :] = high
    payload[panels + rank :, :] = (weights - high.astype(jnp.float32)).astype(payload.dtype)


def to_other_sub(index, keep, taken, panels):
    rows, width = keep.shape
    rank = (rows - panels) // 2
    return pl.pallas_call(
        merge_kernel,
        out_shape=(
            jax.ShapeDtypeStruct((rows, width), jnp.bfloat16),
            jax.ShapeDtypeStruct((2, rank, width), jnp.float32),
        ),
        in_specs=[SMEM, VMEM, VMEM],
        out_specs=(VMEM, VMEM),
        compiler_params=ROOM,
    )(index, keep, taken)


def own_kernel(starts, index, block, full, total):
    forward_rows((0,), index, starts, block, full, total)


def forward_own(index, starts, block, full, width):
    pairs, full_panels, panels = block.shape
    return pl.pallas_call(
        functools.partial(own_kernel, starts),
        out_shape=jax.ShapeDtypeStruct((2, panels, width), jnp.float32),
        in_specs=[SMEM, VMEM, VMEM],
        out_specs=VMEM,
        compiler_params=ROOM,
    )(index, block, full)


def finish_kernel(counts, index, packed, *refs):
    refs = list(refs)
    both, backs, nears, fars, subs = (
        [refs.pop(0) for _ in range(count)] for count in counts
    )
    result, back, weight = refs
    core = index[2]
    clusters, rows, panels = packed.shape
    width = result.shape[2]
    rank = rows - width
    for k, at in enumerate((core, 1 - core)):
        half = len(backs) // 2
        back[at] = sum(term[0].astype(jnp.float32) for term in backs[k * half : (k + 1) * half])
        result[at] = sum(term[at] for term in nears)
        weight[at] = sum(term[at] for term in fars)
        if subs:
            got = subs[k]
            result[at] += got[:panels].astype(jnp.float32)
            weight[at] += got[panels : panels + rank].astype(jnp.float32) + got[
                panels + rank :
            ].astype(jnp.float32)
    for term in both:
        back[...] += term[...].astype(jnp.float32)
    for c in range(clusters):
        for i in range(width // panels):
            weight[c, :, i * panels : (i + 1) * panels] += back[
                c, width + i * rank : width + (i + 1) * rank, :
            ]
        result[c] += back[c, :width, :].T + lax.dot_general(
            packed[c, width:, :].astype(jnp.float32),
            weight[c],
            FIRST,
            precision=HIGHEST,
            preferred_element_type=jnp.float32,
        )


def finish(index, packed, both, backs, nears, fars, subs):
    clusters = packed.shape[0]
    groups = (both, backs[0] + backs[1], nears, fars, subs)
    return pl.pallas_call(
        functools.partial(finish_kernel, tuple(len(group) for group in groups)),
        out_shape=jax.ShapeDtypeStruct(nears[0].shape, jnp.float32),
        in_specs=[SMEM] + [VMEM] * (1 + sum(len(group) for group in groups)),
        out_specs=VMEM,
        scratch_shapes=[
            pltpu.VMEM((clusters,) + backs[0][0].shape[1:], jnp.float32),
            pltpu.VMEM(fars[0].shape, jnp.float32),
        ],
        compiler_params=ROOM,
    )(index, packed, *[array for group in groups for array in group])


def swap(value, axis):
    return lax.ppermute(value, axis, [(0, 1), (1, 0)])


def stage(apart, run, *operands):
    shapes = jax.eval_shape(run, *operands)
    return lax.cond(
        apart,
        run,
        lambda *_: jax.tree.map(lambda v: jnp.zeros(v.shape, v.dtype), shapes),
        *operands,
    )


def index_table(where, *columns):
    starts, at = [], where.shape[0]
    for column in columns:
        starts.append(at)
        at += column.shape[0]
    return jnp.concatenate([where, *columns]), starts


def shards_small(panel_field, near_row, near_col, near_block, bases, far_row, far_col, coupling):
    owner, sub, core = lax.axis_index("clu"), lax.axis_index("sub"), lax.axis_index("rep")
    where = jnp.stack([owner, sub, core]).astype(jnp.int32)
    _, panels, width = panel_field.shape
    rank = bases.shape[2]
    packed, mine = pack(where, panel_field, jnp.swapaxes(bases, 1, 2))

    axes = ("clu", "sub", "rep")
    numbered = [(o, s, r) for o in range(4) for s in range(2) for r in range(2)]
    by_core = [(i, ((o ^ (1 + r)) * 2 + s) * 2 + r) for i, (o, s, r) in enumerate(numbered)]
    opposite = [(o, o ^ 3) for o in range(4)]

    def spread(two, one):
        return lax.ppermute(two, axes, by_core), lax.ppermute(one, "clu", opposite)

    across = swap(mine, "sub")
    first, second = spread(packed, mine)
    held = near_block

    def slot_of(cluster, owner, core):
        turn = lax.shift_right_logical(cluster, 1) ^ owner
        local = cluster & 1
        paired = (turn == 1) | (turn == 2)
        kept = jnp.where(paired, turn == 1 + core, local == core)
        within = jnp.where(paired, local, jnp.where(turn == 3, 2, 3))
        return jnp.where(kept, within, 4 + within)

    index, starts = index_table(where, near_row, near_col, far_row, far_col)
    apart = near_row[0] >= 0

    def back_half(packed, across, coupling, block):
        across_other = swap(across, "rep")
        total = back_sums(
            8,
            slot_of,
            [
                (packed, lambda o, s, r: (0, s)),
                (across, lambda o, s, r: (r, 1 - s)),
                (across_other, lambda o, s, r: (1 - r, 1 - s)),
            ],
            index,
            starts,
            coupling,
            block,
        )
        taken = swap(total[4:], "rep")
        to_two = (total[:2] + taken[:2]).astype(jnp.bfloat16)
        to_one = (total[2:3] + taken[2:3]).astype(jnp.bfloat16)
        return to_two, to_one, total[3:4] + taken[3:]

    to_two, to_one, own = stage(apart, back_half, packed, across, coupling, near_block)
    to_two, to_one, first, second = lax.optimization_barrier((to_two, to_one, first, second))
    back_two, back_one = spread(to_two, to_one)

    def forward_half(packed, first, second, coupling, block):
        first_other, second_other = swap(first, "rep"), swap(second, "rep")
        held = load(block)
        ahead, behind, full = forward_far(
            8,
            [
                (packed, lambda o, s, r: 2 * o),
                (first, lambda o, s, r: 2 * (o ^ (1 + r))),
                (first_other, lambda o, s, r: 2 * (o ^ (2 - r))),
                (second, lambda o, s, r: 2 * (o ^ 3) + r),
                (second_other, lambda o, s, r: 2 * (o ^ 3) + 1 - r),
            ],
            index,
            starts,
            coupling,
            held,
        )
        own_rows = forward_own(index, starts, held, full, width)
        payload, far = to_other_sub(index, ahead, swap(behind, "rep"), panels)
        return payload, far, own_rows

    payload, far, own_rows = stage(apart, forward_half, packed, first, second, coupling, near_block)

    def between_subs(payload, own_rows, own):
        from_sub = swap(payload, "sub")
        own_rows_other, own_other = swap(own_rows, "rep"), swap(own, "rep")
        return from_sub, swap(from_sub, "rep"), own_rows_other, own_other

    from_sub, from_sub_other, own_rows_other, own_other = stage(
        apart, between_subs, payload, own_rows, own
    )
    back_two, back_one, own_other = lax.optimization_barrier((back_two, back_one, own_other))
    back_two_other, back_one_other = swap(back_two, "rep"), swap(back_one, "rep")
    return finish(
        index,
        packed,
        (back_two, back_two_other),
        ((own, back_one), (own_other, back_one_other)),
        (own_rows, own_rows_other),
        (far,),
        (from_sub, from_sub_other),
    )


def shards_any(panel_field, near_row, near_col, near_block, bases, far_row, far_col, coupling):
    owner, sub, core = lax.axis_index("clu"), lax.axis_index("sub"), lax.axis_index("rep")
    owners, subs = lax.axis_size("clu"), lax.axis_size("sub")
    where = jnp.stack([owner, sub, core]).astype(jnp.int32)
    clusters, panels, width = panel_field.shape
    packed, _ = pack(where, panel_field, jnp.swapaxes(bases, 1, 2))
    around = lax.all_gather(packed, "sub", axis=0)
    gathered = lax.all_gather(packed, "clu", axis=0, tiled=True)
    slots = owners * clusters
    index, starts = index_table(where, near_row, near_col, far_row, far_col)
    held = load(near_block)
    back = back_sums(
        slots,
        lambda cluster, owner, core: cluster,
        [(around[k], lambda o, s, r, k=k: (0, k)) for k in range(subs)],
        index,
        starts,
        coupling,
        near_block,
    )
    back = lax.psum(lax.psum_scatter(back, "clu", scatter_dimension=0, tiled=True), "rep")
    ahead, behind, full = forward_far(
        slots, [(gathered, lambda o, s, r: 0)], index, starts, coupling, held
    )
    taken = swap(behind, "rep")
    near = forward_own(index, starts, held, full, width)
    near = near + swap(near, "rep")
    far = lax.psum((ahead + taken)[(subs - 1) * panels :], "sub").reshape(clusters, -1, width)
    ahead = (ahead + taken)[: (subs - 1) * panels]
    for turn in range(1, subs):
        got = lax.ppermute(
            ahead[(turn - 1) * panels : turn * panels],
            "sub",
            [(s, (s + turn) % subs) for s in range(subs)],
        )
        near = near + jnp.where(core == 0, jnp.stack([got, swap(got, "rep")]), jnp.stack([swap(got, "rep"), got]))
    single = lax.dynamic_slice_in_dim(back, core, 1, axis=0)
    other = lax.dynamic_slice_in_dim(back, 1 - core, 1, axis=0)
    return finish(
        index,
        packed,
        (),
        ((single,), (other,)),
        (near,),
        (far,),
        (),
    )


def shards(*arrays):
    sizes = tuple(lax.axis_size(axis) for axis in ("clu", "sub", "rep"))
    if sizes == (4, 2, 2):
        return shards_small(*arrays)
    return shards_any(*arrays)


def solution(mesh):
    placed = (
        P(("parts", "clu"), "sub", None),
        P(("parts", "clu", "rep")),
        P(("parts", "clu", "rep")),
        P(("parts", "clu", "rep"), None, "sub"),
        P(("parts", "clu"), "sub", None),
        P(("parts", "clu", "rep")),
        P(("parts", "clu", "rep")),
        P(("parts", "clu", "rep"), None, None),
    )
    return jax.shard_map(
        shards,
        mesh=mesh,
        in_specs=placed,
        out_specs=P(("parts", "clu"), "sub", None),
        check_vma=False,
    )
```

```python
import functools

import jax
import jax.numpy as jnp
from jax import lax
from jax.experimental import pallas as pl
from jax.experimental.pallas import tpu as pltpu
from jax.sharding import PartitionSpec as P

HIGHEST = lax.Precision.HIGHEST
LAST = (((1,), (1,)), ((), ()))
FIRST = (((0,), (0,)), ((), ()))
VMEM = pl.BlockSpec(memory_space=pltpu.VMEM)
SMEM = pl.BlockSpec(memory_space=pltpu.SMEM)
ANY = pl.BlockSpec(memory_space=pl.ANY)
ROOM = pltpu.CompilerParams(vmem_limit_bytes=32 * 1024 * 1024)


def in_hbm(array):
    return pltpu.with_memory_space_constraint(array, pltpu.HBM)


PARTS = 3


def parts_of(block, held, sems):
    pairs = block.shape[0]
    cuts = [pairs * k // PARTS for k in range(PARTS + 1)]
    return [
        (
            range(a, b),
            pltpu.make_async_copy(block.at[pl.ds(a, b - a)], held.at[pl.ds(a, b - a)], sems.at[k]),
        )
        for k, (a, b) in enumerate(zip(cuts, cuts[1:]))
    ]


def load_kernel(slot_of, starts, index, coupling, block, held, matrix, couplings, table, sems, sem):
    parts = parts_of(block, held, sems)
    first = pltpu.make_async_copy(coupling, couplings, sem)
    first.start()
    for _, copy in parts:
        copy.start()
    table[...] = jnp.zeros_like(table)
    first.wait()
    sum_couplings(slot_of, starts, index, couplings, matrix, table)
    for _, copy in parts:
        copy.wait()


def sum_couplings(slot_of, starts, index, coupling, matrix, table):
    _, _, far_row, far_col = starts
    rank = coupling.shape[1]
    for f in range(coupling.shape[0]):
        at = (index[far_row + f], slot_of(index[far_col + f], index[0], index[2]))
        table[at] = table[at] + coupling[f]
    for c in range(table.shape[0]):
        matrix[c * rank : (c + 1) * rank, :] = jnp.concatenate(
            [table[c, t] for t in range(table.shape[1])], axis=1
        )


def load(slots, slot_of, index, starts, coupling, block):
    rank = coupling.shape[1]
    return pl.pallas_call(
        functools.partial(load_kernel, slot_of, starts),
        out_shape=(
            jax.ShapeDtypeStruct(block.shape, block.dtype),
            jax.ShapeDtypeStruct((2 * rank, slots * rank), jnp.float32),
        ),
        in_specs=[SMEM, ANY, ANY],
        out_specs=(VMEM, VMEM),
        scratch_shapes=[
            pltpu.VMEM(coupling.shape, coupling.dtype),
            pltpu.VMEM((2, slots, rank, rank), jnp.float32),
            pltpu.SemaphoreType.DMA((PARTS,)),
            pltpu.SemaphoreType.DMA,
        ],
        compiler_params=ROOM,
    )(index, in_hbm(coupling), in_hbm(block))


def matrix_kernel(slot_of, starts, index, coupling, matrix, table):
    table[...] = jnp.zeros_like(table)
    sum_couplings(slot_of, starts, index, coupling, matrix, table)


def couplings_by(slots, slot_of, index, starts, coupling):
    rank = coupling.shape[1]
    return pl.pallas_call(
        functools.partial(matrix_kernel, slot_of, starts),
        out_shape=jax.ShapeDtypeStruct((2 * rank, slots * rank), jnp.float32),
        in_specs=[SMEM, VMEM],
        out_specs=VMEM,
        scratch_shapes=[pltpu.VMEM((2, slots, rank, rank), jnp.float32)],
        compiler_params=ROOM,
    )(index, coupling)


def pack_kernel(index, panel, bases, packed, mine, held, sems):
    clusters, _, width = panel.shape
    moves = []
    for c in range(clusters):
        moves.append(pltpu.make_async_copy(panel.at[c], held.at[c], sems.at[2 * c]))
        moves.append(
            pltpu.make_async_copy(bases.at[c], packed.at[c, pl.ds(width, bases.shape[1])], sems.at[2 * c + 1])
        )
    for move in moves:
        move.start()
    for c in range(clusters):
        moves[2 * c].wait()
        packed[c, :width, :] = held[c].T
    for c in range(clusters):
        moves[2 * c + 1].wait()
    mine[0] = packed[index[2]]


def pack(index, panel, bases):
    clusters, panels, width = panel.shape
    rows = width + bases.shape[1]
    return pl.pallas_call(
        pack_kernel,
        out_shape=(
            jax.ShapeDtypeStruct((clusters, rows, panels), panel.dtype),
            jax.ShapeDtypeStruct((1, rows, panels), panel.dtype),
        ),
        in_specs=[SMEM, ANY, ANY],
        out_specs=(VMEM, VMEM),
        scratch_shapes=[
            pltpu.VMEM(panel.shape, panel.dtype),
            pltpu.SemaphoreType.DMA((2 * clusters,)),
        ],
        compiler_params=ROOM,
    )(index, in_hbm(panel), in_hbm(bases))


def each_pair(pairs, step):
    unroll = 13 if pairs % 13 == 0 else 1

    def several(n, carry):
        for k in range(unroll):
            step(n * unroll + k)
        return carry

    lax.fori_loop(0, pairs // unroll, several, 0)


def back_kernel(plan, slot_of, starts, index, matrix, block, *refs):
    n = len(plan)
    pieces = refs[:n]
    total, full = refs[n:]
    near_row, near_col, _, _ = starts
    panels = block.shape[2]
    clusters, rows = full.shape[:2]
    rank = matrix.shape[0] // clusters
    width = rows - rank
    total[:, :width, :] = jnp.zeros((total.shape[0], width, panels), jnp.float32)
    for piece, where in zip(pieces, plan):
        first, sub = where(index[0], index[1], index[2])
        for c in range(piece.shape[0]):
            full[first + c, :, pl.ds(pl.multiple_of(sub * panels, panels), panels)] = piece[c]
    projection = jnp.concatenate(
        [
            lax.dot_general(
                full[c, width:, :], full[c, :width, :], LAST, preferred_element_type=jnp.float32
            )
            for c in range(clusters)
        ],
        axis=0,
    )
    weights = lax.dot_general(
        matrix[...],
        projection,
        FIRST,
        precision=HIGHEST,
        preferred_element_type=jnp.float32,
    )
    for t in range(total.shape[0]):
        for i in range(width // panels):
            total[t, width + i * rank : width + (i + 1) * rank, :] = weights[
                t * rank : (t + 1) * rank, i * panels : (i + 1) * panels
            ]

    def step(q):
        product = jnp.dot(
            full[index[near_row + q], :width, :], block[q], preferred_element_type=jnp.float32
        )
        slot = slot_of(index[near_col + q], index[0], index[2])
        total[slot, :width, :] += product.astype(jnp.bfloat16).astype(jnp.float32)

    each_pair(block.shape[0], step)


def back_sums(slots, slot_of, pieces, index, starts, matrix, block):
    rows = pieces[0][0].shape[1]
    _, full_panels, panels = block.shape
    rank = matrix.shape[1] // slots
    width = rows - rank
    tall = width + rank * (width // panels)
    plan = tuple(where for _, where in pieces)
    return pl.pallas_call(
        functools.partial(back_kernel, plan, slot_of, starts),
        out_shape=jax.ShapeDtypeStruct((slots, tall, panels), jnp.float32),
        in_specs=[SMEM] + [VMEM] * (2 + len(pieces)),
        out_specs=VMEM,
        scratch_shapes=[pltpu.VMEM((2, rows, full_panels), jnp.bfloat16)],
        compiler_params=ROOM,
    )(index, matrix, block, *[p for p, _ in pieces])


def forward_step(turns, index, starts, block, full, total):
    near_row, near_col, _, _ = starts
    rows, panels = total.shape[1] // len(turns), block.shape[2]
    subs = block.shape[1] // panels

    def step(q):
        field = full[index[near_col + q], : total.shape[2], :]
        row = index[near_row + q]
        for k, turn in enumerate(turns):
            at = lax.rem(index[1] + turn, subs)
            product = lax.dot_general(
                block[q, pl.ds(pl.multiple_of(at * panels, panels), panels), :],
                field,
                LAST,
                preferred_element_type=jnp.float32,
            )
            total[row, k * rows : (k + 1) * rows, :] += product

    return step


def forward_kernel(plan, turns, starts, index, matrix, block, *refs):
    n = len(plan)
    pieces = refs[:n]
    keep, give, full, held, total, sems = refs[n:]
    parts = parts_of(block, held, sems)
    for _, copy in parts:
        copy.start()
    slots, rows, _ = full.shape
    rank = matrix.shape[1] // slots
    width = rows - rank
    for piece, where in zip(pieces, plan):
        firsts = where(index[0], index[1], index[2])
        for c, first in enumerate(firsts):
            full[first + c] = piece[c]
    projection = jnp.concatenate(
        [
            lax.dot_general(
                full[t, width:, :], full[t, :width, :], LAST, preferred_element_type=jnp.float32
            )
            for t in range(slots)
        ],
        axis=0,
    )
    weights = jnp.dot(
        matrix[...], projection, precision=HIGHEST, preferred_element_type=jnp.float32
    )
    total[...] = jnp.zeros_like(total)
    step = forward_step(turns, index, starts, held, full, total)
    for pairs, copy in parts:
        copy.wait()
        for q in pairs:
            step(q)
    core, tall = index[2], total.shape[1]
    keep[:tall, :] = total[core]
    keep[tall:, :] = weights
    give[:tall, :] = total[1 - core]
    give[tall:, :] = weights


def forward_far(slots, pieces, index, starts, matrix, block):
    rows = pieces[0][0].shape[1]
    _, full_panels, panels = block.shape
    rank = matrix.shape[1] // slots
    width = rows - rank
    plan = tuple(where for _, where in pieces)
    turns = tuple(range(1, full_panels // panels))
    tall = panels * len(turns)
    shape = jax.ShapeDtypeStruct((tall + 2 * rank, width), jnp.float32)
    return pl.pallas_call(
        functools.partial(forward_kernel, plan, turns, starts),
        out_shape=(
            shape,
            shape,
            jax.ShapeDtypeStruct((slots, rows, panels), jnp.bfloat16),
            jax.ShapeDtypeStruct(block.shape, block.dtype),
        ),
        in_specs=[SMEM, VMEM, ANY] + [VMEM] * len(pieces),
        out_specs=(VMEM,) * 4,
        scratch_shapes=[
            pltpu.VMEM((2, tall, width), jnp.float32),
            pltpu.SemaphoreType.DMA((PARTS,)),
        ],
        compiler_params=ROOM,
    )(index, matrix, in_hbm(block), *[p for p, _ in pieces])


def merge_kernel(index, keep, taken, payload, far):
    rank = far.shape[1]
    panels = keep.shape[0] - 2 * rank
    core = index[2]
    for c in range(2):
        rows = slice(panels + c * rank, panels + (c + 1) * rank)
        far[c] = keep[rows, :] + taken[rows, :]
    weights = far[core]
    high = weights.astype(payload.dtype)
    payload[:panels, :] = (keep[:panels] + taken[:panels]).astype(payload.dtype)
    payload[panels : panels + rank, :] = high
    payload[panels + rank :, :] = (weights - high.astype(jnp.float32)).astype(payload.dtype)


def to_other_sub(index, keep, taken, panels):
    rows, width = keep.shape
    rank = (rows - panels) // 2
    return pl.pallas_call(
        merge_kernel,
        out_shape=(
            jax.ShapeDtypeStruct((rows, width), jnp.bfloat16),
            jax.ShapeDtypeStruct((2, rank, width), jnp.float32),
        ),
        in_specs=[SMEM, VMEM, VMEM],
        out_specs=(VMEM, VMEM),
        compiler_params=ROOM,
    )(index, keep, taken)


def own_kernel(starts, index, block, full, total):
    total[...] = jnp.zeros_like(total)
    each_pair(block.shape[0], forward_step((0,), index, starts, block, full, total))


def forward_own(index, starts, block, full, width):
    return pl.pallas_call(
        functools.partial(own_kernel, starts),
        out_shape=jax.ShapeDtypeStruct((2, block.shape[2], width), jnp.float32),
        in_specs=[SMEM, VMEM, VMEM],
        out_specs=VMEM,
        compiler_params=ROOM,
    )(index, block, full)


def finish_kernel(counts, index, packed, *refs):
    refs = list(refs)
    both, backs, nears, fars, subs = ([refs.pop(0) for _ in range(count)] for count in counts)
    result, back, weight = refs
    core = index[2]
    clusters, rows, panels = packed.shape
    width = result.shape[2]
    rank = rows - width
    half = len(backs) // 2
    for k, at in enumerate((core, 1 - core)):
        back[at] = sum(
            term[0].astype(jnp.float32) for term in backs[k * half : (k + 1) * half]
        )
        near = sum(term[at] for term in nears)
        far = sum(term[at] for term in fars)
        if subs:
            got = subs[k]
            near += got[:panels].astype(jnp.float32)
            far += got[panels : panels + rank].astype(jnp.float32)
            far += got[panels + rank :].astype(jnp.float32)
        result[at] = near
        weight[at] = far
    for term in both:
        back[...] += term[...].astype(jnp.float32)
    for c in range(clusters):
        for i in range(width // panels):
            weight[c, :, i * panels : (i + 1) * panels] += back[
                c, width + i * rank : width + (i + 1) * rank, :
            ]
        result[c] += back[c, :width, :].T + lax.dot_general(
            packed[c, width:, :].astype(jnp.float32),
            weight[c],
            FIRST,
            precision=HIGHEST,
            preferred_element_type=jnp.float32,
        )


def finish(index, packed, both, backs, nears, fars, subs):
    groups = (both, backs[0] + backs[1], nears, fars, subs)
    return pl.pallas_call(
        functools.partial(finish_kernel, tuple(len(group) for group in groups)),
        out_shape=jax.ShapeDtypeStruct(nears[0].shape, jnp.float32),
        in_specs=[SMEM] + [VMEM] * (1 + sum(len(group) for group in groups)),
        out_specs=VMEM,
        scratch_shapes=[
            pltpu.VMEM((packed.shape[0],) + backs[0][0].shape[1:], jnp.float32),
            pltpu.VMEM(fars[0].shape, jnp.float32),
        ],
        compiler_params=ROOM,
    )(index, packed, *[array for group in groups for array in group])


def swap(value, axis):
    return lax.ppermute(value, axis, [(0, 1), (1, 0)])


def stage(apart, run, *operands):
    shapes = jax.eval_shape(run, *operands)
    return lax.cond(
        apart,
        run,
        lambda *_: jax.tree.map(lambda v: jnp.zeros(v.shape, v.dtype), shapes),
        *operands,
    )


def index_table(where, *columns):
    starts, at = [], where.shape[0]
    for column in columns:
        starts.append(at)
        at += column.shape[0]
    return jnp.concatenate([where, *columns]), starts


def shards_small(panel_field, near_row, near_col, near_block, bases, far_row, far_col, coupling):
    owner, sub, core = lax.axis_index("clu"), lax.axis_index("sub"), lax.axis_index("rep")
    where = jnp.stack([owner, sub, core]).astype(jnp.int32)
    _, panels, width = panel_field.shape
    rank = bases.shape[2]
    packed, mine = pack(where, panel_field, jnp.swapaxes(bases, 1, 2))

    axes = ("clu", "sub", "rep")
    numbered = [(o, s, r) for o in range(4) for s in range(2) for r in range(2)]
    by_core = [(i, ((o ^ (1 + r)) * 2 + s) * 2 + r) for i, (o, s, r) in enumerate(numbered)]
    opposite = [(o, o ^ 3) for o in range(4)]

    across = swap(mine, "sub")
    incoming = [lax.ppermute(packed[c : c + 1], axes, by_core) for c in range(2)]
    incoming.append(lax.ppermute(mine, "clu", opposite))
    held = near_block

    def slot_of(cluster, owner, core):
        turn = lax.shift_right_logical(cluster, 1) ^ owner
        local = cluster & 1
        paired = (turn == 1) | (turn == 2)
        kept = jnp.where(paired, turn == 1 + core, local == core)
        within = jnp.where(paired, local, jnp.where(turn == 3, 2, 3))
        return jnp.where(kept, within, 4 + within)

    index, starts = index_table(where, near_row, near_col, far_row, far_col)
    apart = near_row[0] >= 0

    def cluster_of(cluster, owner, core):
        return cluster

    def back_half(packed, across, coupling, block):
        across_other = swap(across, "rep")
        held, by_slot = load(8, slot_of, index, starts, coupling, block)
        total = back_sums(
            8,
            slot_of,
            [
                (packed, lambda o, s, r: (0, s)),
                (across, lambda o, s, r: (r, 1 - s)),
                (across_other, lambda o, s, r: (1 - r, 1 - s)),
            ],
            index,
            starts,
            by_slot,
            held,
        )
        taken = swap(total[4:], "rep")
        to_two = (total[:2] + taken[:2]).astype(jnp.bfloat16)
        to_one = (total[2:3] + taken[2:3]).astype(jnp.bfloat16)
        by_cluster = couplings_by(8, cluster_of, index, starts, coupling)
        return to_two, to_one, total[3:4] + taken[3:], by_cluster

    to_two, to_one, own, by_cluster = stage(
        apart, back_half, packed, across, coupling, near_block
    )
    to_two, to_one, *incoming = lax.optimization_barrier((to_two, to_one, *incoming))
    back_two = lax.ppermute(to_two, axes, by_core)
    back_one = lax.ppermute(to_one, "clu", opposite)
    incoming = jnp.concatenate(incoming, axis=0)
    incoming_other = swap(incoming, "rep")

    def forward_half(packed, incoming, incoming_other, matrix, block):
        ahead, behind, full, held = forward_far(
            8,
            [
                (packed, lambda o, s, r: (2 * o,) * 2),
                (incoming, lambda o, s, r: (2 * (o ^ (1 + r)),) * 2 + (2 * (o ^ 3) + r - 2,)),
                (
                    incoming_other,
                    lambda o, s, r: (2 * (o ^ (2 - r)),) * 2 + (2 * (o ^ 3) + 1 - r - 2,),
                ),
            ],
            index,
            starts,
            matrix,
            block,
        )
        own_rows = forward_own(index, starts, held, full, width)
        payload, far = to_other_sub(index, ahead, swap(behind, "rep"), panels)
        return payload, far, own_rows

    payload, far, own_rows = stage(
        apart, forward_half, packed, incoming, incoming_other, by_cluster, near_block
    )

    def between_subs(payload, own_rows, own):
        own = jnp.where(
            jnp.arange(2)[:, None, None] == core, own, swap(own, "rep")
        )
        return swap(payload, "sub"), own_rows + swap(own_rows, "rep"), own

    from_sub, near, own = stage(apart, between_subs, payload, own_rows, own)
    back_two, back_one, near = lax.optimization_barrier((back_two, back_one, near))
    from_sub_other = swap(from_sub, "rep")
    backs = jnp.concatenate([back_two, back_one], axis=0)
    backs_other = swap(backs, "rep")
    return finish(
        index,
        packed,
        (own, backs[:2], backs_other[:2]),
        ((backs[2:],), (backs_other[2:],)),
        (near,),
        (far,),
        (from_sub, from_sub_other),
    )


def shards_any(panel_field, near_row, near_col, near_block, bases, far_row, far_col, coupling):
    owner, sub, core = lax.axis_index("clu"), lax.axis_index("sub"), lax.axis_index("rep")
    owners, subs = lax.axis_size("clu"), lax.axis_size("sub")
    where = jnp.stack([owner, sub, core]).astype(jnp.int32)
    clusters, panels, width = panel_field.shape
    packed, _ = pack(where, panel_field, jnp.swapaxes(bases, 1, 2))
    around = lax.all_gather(packed, "sub", axis=0)
    gathered = lax.all_gather(packed, "clu", axis=0, tiled=True)
    slots = owners * clusters
    index, starts = index_table(where, near_row, near_col, far_row, far_col)
    def slot_of(cluster, owner, core):
        return cluster

    held, matrix = load(slots, slot_of, index, starts, coupling, near_block)
    back = back_sums(
        slots,
        slot_of,
        [(around[k], lambda o, s, r, k=k: (0, k)) for k in range(subs)],
        index,
        starts,
        matrix,
        held,
    )
    back = lax.psum(lax.psum_scatter(back, "clu", scatter_dimension=0, tiled=True), "rep")
    ahead, behind, full, held = forward_far(
        slots, [(gathered, lambda o, s, r: (0,) * slots)], index, starts, matrix, near_block
    )
    taken = swap(behind, "rep")
    near = forward_own(index, starts, held, full, width)
    near = near + swap(near, "rep")
    far = lax.psum((ahead + taken)[(subs - 1) * panels :], "sub").reshape(clusters, -1, width)
    ahead = (ahead + taken)[: (subs - 1) * panels]
    for turn in range(1, subs):
        got = lax.ppermute(
            ahead[(turn - 1) * panels : turn * panels],
            "sub",
            [(s, (s + turn) % subs) for s in range(subs)],
        )
        near = near + jnp.where(core == 0, jnp.stack([got, swap(got, "rep")]), jnp.stack([swap(got, "rep"), got]))
    single = lax.dynamic_slice_in_dim(back, core, 1, axis=0)
    other = lax.dynamic_slice_in_dim(back, 1 - core, 1, axis=0)
    return finish(index, packed, (), ((single,), (other,)), (near,), (far,), ())


def shards(*arrays):
    sizes = tuple(lax.axis_size(axis) for axis in ("clu", "sub", "rep"))
    if sizes == (4, 2, 2):
        return shards_small(*arrays)
    return shards_any(*arrays)


def solution(mesh):
    placed = (
        P(("parts", "clu"), "sub", None),
        P(("parts", "clu", "rep")),
        P(("parts", "clu", "rep")),
        P(("parts", "clu", "rep"), None, "sub"),
        P(("parts", "clu"), "sub", None),
        P(("parts", "clu", "rep")),
        P(("parts", "clu", "rep")),
        P(("parts", "clu", "rep"), None, None),
    )
    return jax.shard_map(
        shards,
        mesh=mesh,
        in_specs=placed,
        out_specs=P(("parts", "clu"), "sub", None),
        check_vma=False,
    )
```

```python
import functools

import jax
import jax.numpy as jnp
from jax import lax
from jax.experimental import pallas as pl
from jax.experimental.pallas import tpu as pltpu
from jax.sharding import PartitionSpec as P

HIGHEST = lax.Precision.HIGHEST
LAST = (((1,), (1,)), ((), ()))
FIRST = (((0,), (0,)), ((), ()))
VMEM = pl.BlockSpec(memory_space=pltpu.VMEM)
SMEM = pl.BlockSpec(memory_space=pltpu.SMEM)
ANY = pl.BlockSpec(memory_space=pl.ANY)
ROOM = pltpu.CompilerParams(vmem_limit_bytes=32 * 1024 * 1024)


def in_hbm(array):
    return pltpu.with_memory_space_constraint(array, pltpu.HBM)


PARTS = 3


def parts_of(block, held, sems):
    pairs = block.shape[0]
    cuts = [pairs * k // PARTS for k in range(PARTS + 1)]
    return [
        (
            range(a, b),
            pltpu.make_async_copy(block.at[pl.ds(a, b - a)], held.at[pl.ds(a, b - a)], sems.at[k]),
        )
        for k, (a, b) in enumerate(zip(cuts, cuts[1:]))
    ]


def load_kernel(slot_of, starts, index, coupling, block, held, matrix, couplings, table, sems, sem):
    parts = parts_of(block, held, sems)
    first = pltpu.make_async_copy(coupling, couplings, sem)
    first.start()
    for _, copy in parts:
        copy.start()
    table[...] = jnp.zeros_like(table)
    first.wait()
    sum_couplings(slot_of, starts, index, couplings, matrix, table)
    for _, copy in parts:
        copy.wait()


def sum_couplings(slot_of, starts, index, coupling, matrix, table):
    _, _, far_row, far_col = starts
    rank = coupling.shape[1]
    for f in range(coupling.shape[0]):
        at = (index[far_row + f], slot_of(index[far_col + f], index[0], index[2]))
        table[at] = table[at] + coupling[f]
    for c in range(table.shape[0]):
        matrix[c * rank : (c + 1) * rank, :] = jnp.concatenate(
            [table[c, t] for t in range(table.shape[1])], axis=1
        )


def load(slots, slot_of, index, starts, coupling, block):
    rank = coupling.shape[1]
    return pl.pallas_call(
        functools.partial(load_kernel, slot_of, starts),
        out_shape=(
            jax.ShapeDtypeStruct(block.shape, block.dtype),
            jax.ShapeDtypeStruct((2 * rank, slots * rank), jnp.float32),
        ),
        in_specs=[SMEM, ANY, ANY],
        out_specs=(VMEM, VMEM),
        scratch_shapes=[
            pltpu.VMEM(coupling.shape, coupling.dtype),
            pltpu.VMEM((2, slots, rank, rank), jnp.float32),
            pltpu.SemaphoreType.DMA((PARTS,)),
            pltpu.SemaphoreType.DMA,
        ],
        compiler_params=ROOM,
    )(index, in_hbm(coupling), in_hbm(block))


def matrix_kernel(slot_of, starts, index, coupling, matrix, table):
    table[...] = jnp.zeros_like(table)
    sum_couplings(slot_of, starts, index, coupling, matrix, table)


def couplings_by(slots, slot_of, index, starts, coupling):
    rank = coupling.shape[1]
    return pl.pallas_call(
        functools.partial(matrix_kernel, slot_of, starts),
        out_shape=jax.ShapeDtypeStruct((2 * rank, slots * rank), jnp.float32),
        in_specs=[SMEM, VMEM],
        out_specs=VMEM,
        scratch_shapes=[pltpu.VMEM((2, slots, rank, rank), jnp.float32)],
        compiler_params=ROOM,
    )(index, coupling)


def pack_kernel(index, panel, bases, packed, mine, held, sems):
    clusters, _, width = panel.shape
    moves = []
    for c in range(clusters):
        moves.append(pltpu.make_async_copy(panel.at[c], held.at[c], sems.at[2 * c]))
        moves.append(
            pltpu.make_async_copy(bases.at[c], packed.at[c, pl.ds(width, bases.shape[1])], sems.at[2 * c + 1])
        )
    for move in moves:
        move.start()
    for c in range(clusters):
        moves[2 * c].wait()
        packed[c, :width, :] = held[c].T
    for c in range(clusters):
        moves[2 * c + 1].wait()
    mine[0] = packed[index[2]]


def pack(index, panel, bases):
    clusters, panels, width = panel.shape
    rows = width + bases.shape[1]
    return pl.pallas_call(
        pack_kernel,
        out_shape=(
            jax.ShapeDtypeStruct((clusters, rows, panels), panel.dtype),
            jax.ShapeDtypeStruct((1, rows, panels), panel.dtype),
        ),
        in_specs=[SMEM, ANY, ANY],
        out_specs=(VMEM, VMEM),
        scratch_shapes=[
            pltpu.VMEM(panel.shape, panel.dtype),
            pltpu.SemaphoreType.DMA((2 * clusters,)),
        ],
        compiler_params=ROOM,
    )(index, in_hbm(panel), in_hbm(bases))


def each_pair(pairs, step):
    unroll = 13 if pairs % 13 == 0 else 1

    def several(n, carry):
        for k in range(unroll):
            step(n * unroll + k)
        return carry

    lax.fori_loop(0, pairs // unroll, several, 0)


def back_kernel(plan, slot_of, starts, index, matrix, block, *refs):
    n = len(plan)
    pieces = refs[:n]
    total, full = refs[n:]
    near_row, near_col, _, _ = starts
    panels = block.shape[2]
    clusters, rows = full.shape[:2]
    rank = matrix.shape[0] // clusters
    width = rows - rank
    total[:, :width, :] = jnp.zeros((total.shape[0], width, panels), jnp.float32)
    for piece, where in zip(pieces, plan):
        first, sub = where(index[0], index[1], index[2])
        for c in range(piece.shape[0]):
            full[first + c, :, pl.ds(pl.multiple_of(sub * panels, panels), panels)] = piece[c]
    projection = jnp.concatenate(
        [
            lax.dot_general(
                full[c, width:, :], full[c, :width, :], LAST, preferred_element_type=jnp.float32
            )
            for c in range(clusters)
        ],
        axis=0,
    )
    weights = lax.dot_general(
        matrix[...],
        projection,
        FIRST,
        precision=HIGHEST,
        preferred_element_type=jnp.float32,
    )
    for t in range(total.shape[0]):
        for i in range(width // panels):
            total[t, width + i * rank : width + (i + 1) * rank, :] = weights[
                t * rank : (t + 1) * rank, i * panels : (i + 1) * panels
            ]

    def step(q):
        product = jnp.dot(
            full[index[near_row + q], :width, :], block[q], preferred_element_type=jnp.float32
        )
        slot = slot_of(index[near_col + q], index[0], index[2])
        total[slot, :width, :] += product.astype(jnp.bfloat16).astype(jnp.float32)

    each_pair(block.shape[0], step)


def back_sums(slots, slot_of, pieces, index, starts, matrix, block):
    rows = pieces[0][0].shape[1]
    _, full_panels, panels = block.shape
    rank = matrix.shape[1] // slots
    width = rows - rank
    tall = width + rank * (width // panels)
    plan = tuple(where for _, where in pieces)
    return pl.pallas_call(
        functools.partial(back_kernel, plan, slot_of, starts),
        out_shape=jax.ShapeDtypeStruct((slots, tall, panels), jnp.float32),
        in_specs=[SMEM] + [VMEM] * (2 + len(pieces)),
        out_specs=VMEM,
        scratch_shapes=[pltpu.VMEM((2, rows, full_panels), jnp.bfloat16)],
        compiler_params=ROOM,
    )(index, matrix, block, *[p for p, _ in pieces])


def forward_step(turns, index, starts, block, full, total):
    near_row, near_col, _, _ = starts
    rows, panels = total.shape[1] // len(turns), block.shape[2]
    subs = block.shape[1] // panels

    def step(q):
        field = full[index[near_col + q], : total.shape[2], :]
        row = index[near_row + q]
        for k, turn in enumerate(turns):
            at = lax.rem(index[1] + turn, subs)
            product = lax.dot_general(
                block[q, pl.ds(pl.multiple_of(at * panels, panels), panels), :],
                field,
                LAST,
                preferred_element_type=jnp.float32,
            )
            total[row, k * rows : (k + 1) * rows, :] += product

    return step


def forward_kernel(plan, turns, starts, index, matrix, block, *refs):
    n = len(plan)
    pieces = refs[:n]
    keep, give, full, held, total, sems = refs[n:]
    parts = parts_of(block, held, sems)
    for _, copy in parts:
        copy.start()
    slots, rows, _ = full.shape
    rank = matrix.shape[1] // slots
    width = rows - rank
    for piece, where in zip(pieces, plan):
        firsts = where(index[0], index[1], index[2])
        for c, first in enumerate(firsts):
            full[first + c] = piece[c]
    projection = jnp.concatenate(
        [
            lax.dot_general(
                full[t, width:, :], full[t, :width, :], LAST, preferred_element_type=jnp.float32
            )
            for t in range(slots)
        ],
        axis=0,
    )
    weights = jnp.dot(
        matrix[...], projection, precision=HIGHEST, preferred_element_type=jnp.float32
    )
    total[...] = jnp.zeros_like(total)
    step = forward_step(turns, index, starts, held, full, total)
    for pairs, copy in parts:
        copy.wait()
        for q in pairs:
            step(q)
    core, tall = index[2], total.shape[1]
    keep[:tall, :] = total[core]
    keep[tall:, :] = weights
    give[:tall, :] = total[1 - core]
    give[tall:, :] = weights


def forward_far(slots, pieces, index, starts, matrix, block):
    rows = pieces[0][0].shape[1]
    _, full_panels, panels = block.shape
    rank = matrix.shape[1] // slots
    width = rows - rank
    plan = tuple(where for _, where in pieces)
    turns = tuple(range(1, full_panels // panels))
    tall = panels * len(turns)
    shape = jax.ShapeDtypeStruct((tall + 2 * rank, width), jnp.float32)
    return pl.pallas_call(
        functools.partial(forward_kernel, plan, turns, starts),
        out_shape=(
            shape,
            shape,
            jax.ShapeDtypeStruct((slots, rows, panels), jnp.bfloat16),
            jax.ShapeDtypeStruct(block.shape, block.dtype),
        ),
        in_specs=[SMEM, VMEM, ANY] + [VMEM] * len(pieces),
        out_specs=(VMEM,) * 4,
        scratch_shapes=[
            pltpu.VMEM((2, tall, width), jnp.float32),
            pltpu.SemaphoreType.DMA((PARTS,)),
        ],
        compiler_params=ROOM,
    )(index, matrix, in_hbm(block), *[p for p, _ in pieces])


def merge_kernel(index, keep, taken, payload, far):
    rank = far.shape[1]
    panels = keep.shape[0] - 2 * rank
    core = index[2]
    for c in range(2):
        rows = slice(panels + c * rank, panels + (c + 1) * rank)
        far[c] = keep[rows, :] + taken[rows, :]
    weights = far[core]
    high = weights.astype(payload.dtype)
    payload[:panels, :] = (keep[:panels] + taken[:panels]).astype(payload.dtype)
    payload[panels : panels + rank, :] = high
    payload[panels + rank :, :] = (weights - high.astype(jnp.float32)).astype(payload.dtype)


def to_other_sub(index, keep, taken, panels):
    rows, width = keep.shape
    rank = (rows - panels) // 2
    return pl.pallas_call(
        merge_kernel,
        out_shape=(
            jax.ShapeDtypeStruct((rows, width), jnp.bfloat16),
            jax.ShapeDtypeStruct((2, rank, width), jnp.float32),
        ),
        in_specs=[SMEM, VMEM, VMEM],
        out_specs=(VMEM, VMEM),
        compiler_params=ROOM,
    )(index, keep, taken)


def own_kernel(starts, index, block, full, total):
    total[...] = jnp.zeros_like(total)
    each_pair(block.shape[0], forward_step((0,), index, starts, block, full, total))


def forward_own(index, starts, block, full, width):
    return pl.pallas_call(
        functools.partial(own_kernel, starts),
        out_shape=jax.ShapeDtypeStruct((2, block.shape[2], width), jnp.float32),
        in_specs=[SMEM, VMEM, VMEM],
        out_specs=VMEM,
        compiler_params=ROOM,
    )(index, block, full)


def finish_kernel(counts, index, packed, *refs):
    refs = list(refs)
    both, backs, nears, fars, subs = ([refs.pop(0) for _ in range(count)] for count in counts)
    result, back, weight = refs
    core = index[2]
    clusters, rows, panels = packed.shape
    width = result.shape[2]
    rank = rows - width
    half = len(backs) // 2
    for k, at in enumerate((core, 1 - core)):
        back[at] = sum(
            term[0].astype(jnp.float32) for term in backs[k * half : (k + 1) * half]
        )
        near = sum(term[at] for term in nears)
        far = sum(term[at] for term in fars)
        if subs:
            got = subs[k]
            near += got[:panels].astype(jnp.float32)
            far += got[panels : panels + rank].astype(jnp.float32)
            far += got[panels + rank :].astype(jnp.float32)
        result[at] = near
        weight[at] = far
    for term in both:
        back[...] += term[...].astype(jnp.float32)
    for c in range(clusters):
        for i in range(width // panels):
            weight[c, :, i * panels : (i + 1) * panels] += back[
                c, width + i * rank : width + (i + 1) * rank, :
            ]
        result[c] += back[c, :width, :].T + lax.dot_general(
            packed[c, width:, :].astype(jnp.float32),
            weight[c],
            FIRST,
            precision=HIGHEST,
            preferred_element_type=jnp.float32,
        )


def finish(index, packed, both, backs, nears, fars, subs):
    groups = (both, backs[0] + backs[1], nears, fars, subs)
    return pl.pallas_call(
        functools.partial(finish_kernel, tuple(len(group) for group in groups)),
        out_shape=jax.ShapeDtypeStruct(nears[0].shape, jnp.float32),
        in_specs=[SMEM] + [VMEM] * (1 + sum(len(group) for group in groups)),
        out_specs=VMEM,
        scratch_shapes=[
            pltpu.VMEM((packed.shape[0],) + backs[0][0].shape[1:], jnp.float32),
            pltpu.VMEM(fars[0].shape, jnp.float32),
        ],
        compiler_params=ROOM,
    )(index, packed, *[array for group in groups for array in group])


def swap(value, axis):
    return lax.ppermute(value, axis, [(0, 1), (1, 0)])


def stage(apart, run, *operands):
    shapes = jax.eval_shape(run, *operands)
    return lax.cond(
        apart,
        run,
        lambda *_: jax.tree.map(lambda v: jnp.zeros(v.shape, v.dtype), shapes),
        *operands,
    )


def index_table(where, *columns):
    starts, at = [], where.shape[0]
    for column in columns:
        starts.append(at)
        at += column.shape[0]
    return jnp.concatenate([where, *columns]), starts


def shards_small(panel_field, near_row, near_col, near_block, bases, far_row, far_col, coupling):
    owner, sub, core = lax.axis_index("clu"), lax.axis_index("sub"), lax.axis_index("rep")
    where = jnp.stack([owner, sub, core]).astype(jnp.int32)
    _, panels, width = panel_field.shape
    rank = bases.shape[2]
    packed, mine = pack(where, panel_field, jnp.swapaxes(bases, 1, 2))

    axes = ("clu", "sub", "rep")
    numbered = [(o, s, r) for o in range(4) for s in range(2) for r in range(2)]
    by_core = [(i, ((o ^ (1 + r)) * 2 + s) * 2 + r) for i, (o, s, r) in enumerate(numbered)]
    opposite = [(o, o ^ 3) for o in range(4)]

    across = swap(mine, "sub")
    incoming = [lax.ppermute(packed[c : c + 1], axes, by_core) for c in range(2)]
    incoming.append(lax.ppermute(mine, "clu", opposite))
    held = near_block

    def slot_of(cluster, owner, core):
        turn = lax.shift_right_logical(cluster, 1) ^ owner
        local = cluster & 1
        paired = (turn == 1) | (turn == 2)
        kept = jnp.where(paired, turn == 1 + core, local == core)
        within = jnp.where(paired, local, jnp.where(turn == 3, 2, 3))
        return jnp.where(kept, within, 4 + within)

    index, starts = index_table(where, near_row, near_col, far_row, far_col)
    apart = where[0] >= 0

    def cluster_of(cluster, owner, core):
        return cluster

    def back_half(packed, across, coupling, block):
        across_other = swap(across, "rep")
        held, by_slot = load(8, slot_of, index, starts, coupling, block)
        total = back_sums(
            8,
            slot_of,
            [
                (packed, lambda o, s, r: (0, s)),
                (across, lambda o, s, r: (r, 1 - s)),
                (across_other, lambda o, s, r: (1 - r, 1 - s)),
            ],
            index,
            starts,
            by_slot,
            held,
        )
        taken = swap(total[4:], "rep")
        to_two = (total[:2] + taken[:2]).astype(jnp.bfloat16)
        to_one = (total[2:3] + taken[2:3]).astype(jnp.bfloat16)
        by_cluster = couplings_by(8, cluster_of, index, starts, coupling)
        return to_two, to_one, total[3:4] + taken[3:], by_cluster

    to_two, to_one, own, by_cluster = stage(
        apart, back_half, packed, across, coupling, near_block
    )
    to_two, *pair = lax.optimization_barrier((to_two, *incoming[:2]))
    to_one, *incoming = lax.optimization_barrier((to_one, *pair, incoming[2]))
    back_two = lax.ppermute(to_two, axes, by_core)
    back_one = lax.ppermute(to_one, "clu", opposite)
    incoming = jnp.concatenate(incoming, axis=0)
    incoming_other = swap(incoming, "rep")

    def forward_half(packed, incoming, incoming_other, matrix, block):
        ahead, behind, full, held = forward_far(
            8,
            [
                (packed, lambda o, s, r: (2 * o,) * 2),
                (incoming, lambda o, s, r: (2 * (o ^ (1 + r)),) * 2 + (2 * (o ^ 3) + r - 2,)),
                (
                    incoming_other,
                    lambda o, s, r: (2 * (o ^ (2 - r)),) * 2 + (2 * (o ^ 3) + 1 - r - 2,),
                ),
            ],
            index,
            starts,
            matrix,
            block,
        )
        own_rows = forward_own(index, starts, held, full, width)
        payload, far = to_other_sub(index, ahead, swap(behind, "rep"), panels)
        return payload, far, own_rows

    payload, far, own_rows = stage(
        apart, forward_half, packed, incoming, incoming_other, by_cluster, near_block
    )

    from_sub = swap(payload, "sub")
    backs = jnp.concatenate([back_two, back_one], axis=0)
    backs_other = swap(backs, "rep")
    own_other, own_rows_other = swap(own, "rep"), swap(own_rows, "rep")
    from_sub_other = swap(from_sub.astype(jnp.float32), "rep")
    return finish(
        index,
        packed,
        (backs[:2], backs_other[:2]),
        ((own, backs[2:]), (own_other, backs_other[2:])),
        (own_rows, own_rows_other),
        (far,),
        (from_sub, from_sub_other),
    )


def shards_any(panel_field, near_row, near_col, near_block, bases, far_row, far_col, coupling):
    owner, sub, core = lax.axis_index("clu"), lax.axis_index("sub"), lax.axis_index("rep")
    owners, subs = lax.axis_size("clu"), lax.axis_size("sub")
    where = jnp.stack([owner, sub, core]).astype(jnp.int32)
    clusters, panels, width = panel_field.shape
    packed, _ = pack(where, panel_field, jnp.swapaxes(bases, 1, 2))
    around = lax.all_gather(packed, "sub", axis=0)
    gathered = lax.all_gather(packed, "clu", axis=0, tiled=True)
    slots = owners * clusters
    index, starts = index_table(where, near_row, near_col, far_row, far_col)
    def slot_of(cluster, owner, core):
        return cluster

    held, matrix = load(slots, slot_of, index, starts, coupling, near_block)
    back = back_sums(
        slots,
        slot_of,
        [(around[k], lambda o, s, r, k=k: (0, k)) for k in range(subs)],
        index,
        starts,
        matrix,
        held,
    )
    back = lax.psum(lax.psum_scatter(back, "clu", scatter_dimension=0, tiled=True), "rep")
    ahead, behind, full, held = forward_far(
        slots, [(gathered, lambda o, s, r: (0,) * slots)], index, starts, matrix, near_block
    )
    taken = swap(behind, "rep")
    near = forward_own(index, starts, held, full, width)
    near = near + swap(near, "rep")
    far = lax.psum((ahead + taken)[(subs - 1) * panels :], "sub").reshape(clusters, -1, width)
    ahead = (ahead + taken)[: (subs - 1) * panels]
    for turn in range(1, subs):
        got = lax.ppermute(
            ahead[(turn - 1) * panels : turn * panels],
            "sub",
            [(s, (s + turn) % subs) for s in range(subs)],
        )
        near = near + jnp.where(core == 0, jnp.stack([got, swap(got, "rep")]), jnp.stack([swap(got, "rep"), got]))
    single = lax.dynamic_slice_in_dim(back, core, 1, axis=0)
    other = lax.dynamic_slice_in_dim(back, 1 - core, 1, axis=0)
    return finish(index, packed, (), ((single,), (other,)), (near,), (far,), ())


def shards(*arrays):
    sizes = tuple(lax.axis_size(axis) for axis in ("clu", "sub", "rep"))
    if sizes == (4, 2, 2):
        return shards_small(*arrays)
    return shards_any(*arrays)


def solution(mesh):
    placed = (
        P(("parts", "clu"), "sub", None),
        P(("parts", "clu", "rep")),
        P(("parts", "clu", "rep")),
        P(("parts", "clu", "rep"), None, "sub"),
        P(("parts", "clu"), "sub", None),
        P(("parts", "clu", "rep")),
        P(("parts", "clu", "rep")),
        P(("parts", "clu", "rep"), None, None),
    )
    return jax.shard_map(
        shards,
        mesh=mesh,
        in_specs=placed,
        out_specs=P(("parts", "clu"), "sub", None),
        check_vma=False,
    )
```

```python
import functools

import jax
import jax.numpy as jnp
from jax import lax
from jax.experimental import pallas as pl
from jax.experimental.pallas import tpu as pltpu
from jax.sharding import PartitionSpec as P

LAST = (((1,), (1,)), ((), ()))
FIRST = (((0,), (0,)), ((), ()))
VMEM = pl.BlockSpec(memory_space=pltpu.VMEM)
SMEM = pl.BlockSpec(memory_space=pltpu.SMEM)
ANY = pl.BlockSpec(memory_space=pl.ANY)
ROOM = pltpu.CompilerParams(vmem_limit_bytes=32 * 1024 * 1024)


def in_hbm(array):
    return pltpu.with_memory_space_constraint(array, pltpu.HBM)


PARTS = 4


class Scalars:
    def __init__(self, sources, held, sems):
        self.held = held
        self.copies = [
            pltpu.make_async_copy(source, target, sems.at[k])
            for k, (source, target) in enumerate(zip(sources, held))
        ]
        for copy in self.copies:
            copy.start()

    def wait(self):
        for copy in self.copies:
            copy.wait()
        return self.held


def scalar_scratch(*arrays):
    return [pltpu.SMEM(array.shape, jnp.int32) for array in arrays] + [
        pltpu.SemaphoreType.DMA((len(arrays),))
    ]


def parts_of(block, held, sems):
    pairs = block.shape[0]
    cuts = [pairs * k // PARTS for k in range(PARTS + 1)]
    return [
        (
            range(a, b),
            pltpu.make_async_copy(block.at[pl.ds(a, b - a)], held.at[pl.ds(a, b - a)], sems.at[k]),
        )
        for k, (a, b) in enumerate(zip(cuts, cuts[1:]))
    ]


def load_kernel(far_row, far_col, coupling, block, held, matrix, couplings, table, sems, sem, *scratch):
    parts = parts_of(block, held, sems)
    for _, copy in parts:
        copy.start()
    first = pltpu.make_async_copy(coupling, couplings, sem)
    first.start()
    scalars = Scalars((far_row, far_col), scratch[:2], scratch[2])
    table[...] = jnp.zeros_like(table)
    rows, columns = scalars.wait()
    first.wait()
    sum_couplings(rows, columns, couplings, matrix, table)
    for _, copy in parts:
        copy.wait()


def sum_couplings(far_row, far_col, coupling, matrix, table):
    rank = coupling.shape[1]
    for f in range(coupling.shape[0]):
        at = (far_row[f], far_col[f])
        table[at] = table[at] + coupling[f]
    for c in range(table.shape[0]):
        matrix[c * rank : (c + 1) * rank, :] = jnp.concatenate(
            [table[c, t] for t in range(table.shape[1])], axis=1
        )


def load(slots, far_row, far_col, coupling, block):
    rank = coupling.shape[1]
    return pl.pallas_call(
        load_kernel,
        out_shape=(
            jax.ShapeDtypeStruct(block.shape, block.dtype),
            jax.ShapeDtypeStruct((2 * rank, slots * rank), jnp.float32),
        ),
        in_specs=[ANY] * 4,
        out_specs=(VMEM, VMEM),
        scratch_shapes=[
            pltpu.VMEM(coupling.shape, coupling.dtype),
            pltpu.VMEM((2, slots, rank, rank), jnp.float32),
            pltpu.SemaphoreType.DMA((PARTS,)),
            pltpu.SemaphoreType.DMA,
            *scalar_scratch(far_row, far_col),
        ],
        compiler_params=ROOM,
    )(in_hbm(far_row), in_hbm(far_col), in_hbm(coupling), in_hbm(block))


def pack_kernel(index, panel, bases, packed, mine, held, sems):
    clusters, _, width = panel.shape
    moves = []
    for c in range(clusters):
        moves.append(pltpu.make_async_copy(panel.at[c], held.at[c], sems.at[2 * c]))
        moves.append(
            pltpu.make_async_copy(bases.at[c], packed.at[c, pl.ds(width, bases.shape[1])], sems.at[2 * c + 1])
        )
    for move in moves:
        move.start()
    for c in range(clusters):
        moves[2 * c].wait()
        packed[c, :width, :] = held[c].T
    for c in range(clusters):
        moves[2 * c + 1].wait()
    mine[0] = packed[index[2]]


def pack(index, panel, bases):
    clusters, panels, width = panel.shape
    rows = width + bases.shape[1]
    return pl.pallas_call(
        pack_kernel,
        out_shape=(
            jax.ShapeDtypeStruct((clusters, rows, panels), panel.dtype),
            jax.ShapeDtypeStruct((1, rows, panels), panel.dtype),
        ),
        in_specs=[SMEM, ANY, ANY],
        out_specs=(VMEM, VMEM),
        scratch_shapes=[
            pltpu.VMEM(panel.shape, panel.dtype),
            pltpu.SemaphoreType.DMA((2 * clusters,)),
        ],
        compiler_params=ROOM,
    )(index, in_hbm(panel), in_hbm(bases))


def parts_in_bfloat16(value, count):
    out = []
    for _ in range(count):
        out.append(value.astype(jnp.bfloat16))
        value = value - out[-1].astype(jnp.float32)
    return out


def product_in_parts(left, right, dims):
    (inner_left,), (inner_right,) = dims[0]
    left_high, left_low = parts_in_bfloat16(left, 2)
    right_high, right_low = parts_in_bfloat16(right, 2)
    return lax.dot_general(
        jnp.concatenate([left_high, left_high, left_low], axis=inner_left),
        jnp.concatenate([right_high, right_low, right_high], axis=inner_right),
        dims,
        preferred_element_type=jnp.float32,
    )


def each_pair(pairs, step):
    for q in range(pairs):
        step(q)


def back_kernel(plan, slot_of, where, near_row, near_col, matrix, block, *refs):
    n = len(plan)
    pieces = refs[:n]
    total, full, *scratch = refs[n:]
    scalars = Scalars((where, near_row, near_col), scratch[:3], scratch[3])
    panels = block.shape[2]
    clusters, rows = full.shape[:2]
    rank = matrix.shape[0] // clusters
    width = rows - rank
    total[:, :width, :] = jnp.zeros((total.shape[0], width, panels), jnp.float32)
    index, near_row, near_col = scalars.wait()
    for piece, where in zip(pieces, plan):
        first, sub = where(index[0], index[1], index[2])
        for c in range(piece.shape[0]):
            full[first + c, :, pl.ds(pl.multiple_of(sub * panels, panels), panels)] = piece[c]
    projection = jnp.concatenate(
        [
            lax.dot_general(
                full[c, width:, :], full[c, :width, :], LAST, preferred_element_type=jnp.float32
            )
            for c in range(clusters)
        ],
        axis=0,
    )
    weights = product_in_parts(matrix[...], projection, FIRST)
    for t in range(total.shape[0]):
        slot = slot_of(t, index[0], index[2])
        for i in range(width // panels):
            total[slot, width + i * rank : width + (i + 1) * rank, :] = weights[
                t * rank : (t + 1) * rank, i * panels : (i + 1) * panels
            ]

    def step(q):
        product = jnp.dot(
            full[near_row[q], :width, :], block[q], preferred_element_type=jnp.float32
        )
        slot = slot_of(near_col[q], index[0], index[2])
        total[slot, :width, :] += product.astype(jnp.bfloat16).astype(jnp.float32)

    each_pair(block.shape[0], step)


def back_sums(slots, slot_of, pieces, where, near_row, near_col, matrix, block):
    rows = pieces[0][0].shape[1]
    _, full_panels, panels = block.shape
    rank = matrix.shape[1] // slots
    width = rows - rank
    tall = width + rank * (width // panels)
    plan = tuple(where for _, where in pieces)
    return pl.pallas_call(
        functools.partial(back_kernel, plan, slot_of),
        out_shape=jax.ShapeDtypeStruct((slots, tall, panels), jnp.float32),
        in_specs=[ANY] * 3 + [VMEM] * (2 + len(pieces)),
        out_specs=VMEM,
        scratch_shapes=[
            pltpu.VMEM((2, rows, full_panels), jnp.bfloat16),
            *scalar_scratch(where, near_row, near_col),
        ],
        compiler_params=ROOM,
    )(where, in_hbm(near_row), in_hbm(near_col), matrix, block, *[p for p, _ in pieces])


def forward_step(turns, index, near_row, near_col, block, full, total):
    rows, panels = total.shape[1] // len(turns), block.shape[2]
    subs = block.shape[1] // panels

    def step(q):
        field = full[near_col[q], : total.shape[2], :]
        row = near_row[q]
        for k, turn in enumerate(turns):
            at = lax.rem(index[1] + turn, subs)
            product = lax.dot_general(
                block[q, pl.ds(pl.multiple_of(at * panels, panels), panels), :],
                field,
                LAST,
                preferred_element_type=jnp.float32,
            )
            total[row, k * rows : (k + 1) * rows, :] += product

    return step


def forward_kernel(plan, turns, where, near_row, near_col, matrix, block, *refs):
    n = len(plan)
    pieces = refs[:n]
    keep, give, full, held, total, sems, *scratch = refs[n:]
    scalars = Scalars((where, near_row, near_col), scratch[:3], scratch[3])
    parts = parts_of(block, held, sems)
    for _, copy in parts:
        copy.start()
    slots, rows, _ = full.shape
    rank = matrix.shape[1] // slots
    width = rows - rank
    total[...] = jnp.zeros_like(total)
    index, near_row, near_col = scalars.wait()
    for piece, where in zip(pieces, plan):
        firsts = where(index[0], index[1], index[2])
        for c, first in enumerate(firsts):
            full[first + c] = piece[c]
    projection = jnp.concatenate(
        [
            lax.dot_general(
                full[t, width:, :], full[t, :width, :], LAST, preferred_element_type=jnp.float32
            )
            for t in range(slots)
        ],
        axis=0,
    )
    weights = product_in_parts(matrix[...], projection, (((1,), (0,)), ((), ())))
    step = forward_step(turns, index, near_row, near_col, held, full, total)
    for pairs, copy in parts:
        copy.wait()
        for q in pairs:
            step(q)
    core, tall = index[2], total.shape[1]
    keep[:tall, :] = total[core]
    keep[tall:, :] = weights
    give[:tall, :] = total[1 - core]
    give[tall:, :] = weights


def forward_far(slots, pieces, where, near_row, near_col, matrix, block):
    rows = pieces[0][0].shape[1]
    _, full_panels, panels = block.shape
    rank = matrix.shape[1] // slots
    width = rows - rank
    plan = tuple(where for _, where in pieces)
    turns = tuple(range(1, full_panels // panels))
    tall = panels * len(turns)
    shape = jax.ShapeDtypeStruct((tall + 2 * rank, width), jnp.float32)
    return pl.pallas_call(
        functools.partial(forward_kernel, plan, turns),
        out_shape=(
            shape,
            shape,
            jax.ShapeDtypeStruct((slots, rows, panels), jnp.bfloat16),
            jax.ShapeDtypeStruct(block.shape, block.dtype),
        ),
        in_specs=[ANY] * 3 + [VMEM, ANY] + [VMEM] * len(pieces),
        out_specs=(VMEM,) * 4,
        scratch_shapes=[
            pltpu.VMEM((2, tall, width), jnp.float32),
            pltpu.SemaphoreType.DMA((PARTS,)),
            *scalar_scratch(where, near_row, near_col),
        ],
        compiler_params=ROOM,
    )(where, in_hbm(near_row), in_hbm(near_col), matrix, in_hbm(block), *[p for p, _ in pieces])


def merge_kernel(index, keep, taken, payload, far):
    rank = far.shape[1]
    panels = keep.shape[0] - 2 * rank
    core = index[2]
    for c in range(2):
        rows = slice(panels + c * rank, panels + (c + 1) * rank)
        far[c] = keep[rows, :] + taken[rows, :]
    weights = far[core]
    high = weights.astype(payload.dtype)
    payload[:panels, :] = (keep[:panels] + taken[:panels]).astype(payload.dtype)
    payload[panels : panels + rank, :] = high
    payload[panels + rank :, :] = (weights - high.astype(jnp.float32)).astype(payload.dtype)


def to_other_sub(index, keep, taken, panels):
    rows, width = keep.shape
    rank = (rows - panels) // 2
    return pl.pallas_call(
        merge_kernel,
        out_shape=(
            jax.ShapeDtypeStruct((rows, width), jnp.bfloat16),
            jax.ShapeDtypeStruct((2, rank, width), jnp.float32),
        ),
        in_specs=[SMEM, VMEM, VMEM],
        out_specs=(VMEM, VMEM),
        compiler_params=ROOM,
    )(index, keep, taken)


def own_kernel(where, near_row, near_col, block, full, total, *scratch):
    scalars = Scalars((where, near_row, near_col), scratch[:3], scratch[3])
    total[...] = jnp.zeros_like(total)
    index, near_row, near_col = scalars.wait()
    each_pair(
        block.shape[0], forward_step((0,), index, near_row, near_col, block, full, total)
    )


def forward_own(where, near_row, near_col, block, full, width):
    return pl.pallas_call(
        own_kernel,
        out_shape=jax.ShapeDtypeStruct((2, block.shape[2], width), jnp.float32),
        in_specs=[ANY] * 3 + [VMEM, VMEM],
        out_specs=VMEM,
        scratch_shapes=scalar_scratch(where, near_row, near_col),
        compiler_params=ROOM,
    )(where, in_hbm(near_row), in_hbm(near_col), block, full)


def finish_kernel(counts, index, packed, *refs):
    refs = list(refs)
    both, backs, nears, fars, subs = ([refs.pop(0) for _ in range(count)] for count in counts)
    result, back, weight = refs
    core = index[2]
    clusters, rows, panels = packed.shape
    width = result.shape[2]
    rank = rows - width
    half = len(backs) // 2
    for k, at in enumerate((core, 1 - core)):
        back[at] = sum(
            term[0].astype(jnp.float32) for term in backs[k * half : (k + 1) * half]
        )
        near = sum(term[at] for term in nears)
        far = sum(term[at] for term in fars)
        if subs:
            got = subs[k]
            near += got[:panels].astype(jnp.float32)
            far += got[panels : panels + rank].astype(jnp.float32)
            far += got[panels + rank :].astype(jnp.float32)
        result[at] = near
        weight[at] = far
    for term in both:
        back[...] += term[...].astype(jnp.float32)
    for c in range(clusters):
        for i in range(width // panels):
            weight[c, :, i * panels : (i + 1) * panels] += back[
                c, width + i * rank : width + (i + 1) * rank, :
            ]
        result[c] += back[c, :width, :].T + lax.dot_general(
            jnp.concatenate([packed[c, width:, :]] * 3, axis=0),
            jnp.concatenate(parts_in_bfloat16(weight[c], 3), axis=0),
            FIRST,
            preferred_element_type=jnp.float32,
        )


def finish(index, packed, both, backs, nears, fars, subs):
    groups = (both, backs[0] + backs[1], nears, fars, subs)
    return pl.pallas_call(
        functools.partial(finish_kernel, tuple(len(group) for group in groups)),
        out_shape=jax.ShapeDtypeStruct(nears[0].shape, jnp.float32),
        in_specs=[SMEM] + [VMEM] * (1 + sum(len(group) for group in groups)),
        out_specs=VMEM,
        scratch_shapes=[
            pltpu.VMEM((packed.shape[0],) + backs[0][0].shape[1:], jnp.float32),
            pltpu.VMEM(fars[0].shape, jnp.float32),
        ],
        compiler_params=ROOM,
    )(index, packed, *[array for group in groups for array in group])


def swap(value, axis):
    return lax.ppermute(value, axis, [(0, 1), (1, 0)])


def stage(apart, run, *operands):
    shapes = jax.eval_shape(run, *operands)
    return lax.cond(
        apart,
        run,
        lambda *_: jax.tree.map(lambda v: jnp.zeros(v.shape, v.dtype), shapes),
        *operands,
    )


def shards_small(panel_field, near_row, near_col, near_block, bases, far_row, far_col, coupling):
    owner, sub, core = lax.axis_index("clu"), lax.axis_index("sub"), lax.axis_index("rep")
    where = jnp.stack([owner, sub, core]).astype(jnp.int32)
    _, panels, width = panel_field.shape
    rank = bases.shape[2]
    packed, mine = pack(where, panel_field, jnp.swapaxes(bases, 1, 2))

    axes = ("clu", "sub", "rep")
    numbered = [(o, s, r) for o in range(4) for s in range(2) for r in range(2)]
    by_core = [(i, ((o ^ (1 + r)) * 2 + s) * 2 + r) for i, (o, s, r) in enumerate(numbered)]
    opposite = [(o, o ^ 3) for o in range(4)]

    across = swap(mine, "sub")
    incoming = [lax.ppermute(packed[c : c + 1], axes, by_core) for c in range(2)]
    incoming.append(lax.ppermute(mine, "clu", opposite))
    held = near_block

    def slot_of(cluster, owner, core):
        turn = lax.shift_right_logical(cluster, 1) ^ owner
        local = cluster & 1
        paired = (turn == 1) | (turn == 2)
        kept = jnp.where(paired, turn == 1 + core, local == core)
        within = jnp.where(paired, local, jnp.where(turn == 3, 2, 3))
        return jnp.where(kept, within, 4 + within)

    apart = where[0] >= 0

    def back_half(packed, across, near_row, near_col, far_row, far_col, coupling, block):
        across_other = swap(across, "rep")
        held, matrix = load(8, far_row, far_col, coupling, block)
        total = back_sums(
            8,
            slot_of,
            [
                (packed, lambda o, s, r: (0, s)),
                (across, lambda o, s, r: (r, 1 - s)),
                (across_other, lambda o, s, r: (1 - r, 1 - s)),
            ],
            where,
            near_row,
            near_col,
            matrix,
            held,
        )
        taken = swap(total[4:], "rep")
        to_two = (total[:2] + taken[:2]).astype(jnp.bfloat16)
        to_one = (total[2:3] + taken[2:3]).astype(jnp.bfloat16)
        return to_two, to_one, total[3:4] + taken[3:], matrix

    to_two, to_one, own, matrix = stage(
        apart,
        back_half,
        packed,
        across,
        near_row,
        near_col,
        far_row,
        far_col,
        coupling,
        near_block,
    )
    to_two, *pair = lax.optimization_barrier((to_two, *incoming[:2]))
    to_one, *incoming = lax.optimization_barrier((to_one, *pair, incoming[2]))
    back_two = lax.ppermute(to_two, axes, by_core)
    back_one = lax.ppermute(to_one, "clu", opposite)
    incoming = jnp.concatenate(incoming, axis=0)
    incoming_other = swap(incoming, "rep")

    def forward_half(packed, incoming, incoming_other, matrix, near_row, near_col, block):
        ahead, behind, full, held = forward_far(
            8,
            [
                (packed, lambda o, s, r: (2 * o,) * 2),
                (incoming, lambda o, s, r: (2 * (o ^ (1 + r)),) * 2 + (2 * (o ^ 3) + r - 2,)),
                (
                    incoming_other,
                    lambda o, s, r: (2 * (o ^ (2 - r)),) * 2 + (2 * (o ^ 3) + 1 - r - 2,),
                ),
            ],
            where,
            near_row,
            near_col,
            matrix,
            block,
        )
        own_rows = forward_own(where, near_row, near_col, held, full, width)
        payload, far = to_other_sub(where, ahead, swap(behind, "rep"), panels)
        return payload, far, own_rows

    payload, far, own_rows = stage(
        apart,
        forward_half,
        packed,
        incoming,
        incoming_other,
        matrix,
        near_row,
        near_col,
        near_block,
    )

    from_sub = swap(payload, "sub")
    backs = jnp.concatenate([back_two, back_one], axis=0)
    backs_other = swap(backs, "rep")
    own_other, own_rows_other = swap(own, "rep"), swap(own_rows, "rep")
    own_other, from_sub = lax.optimization_barrier((own_other, from_sub))
    from_sub_other = swap(from_sub.astype(jnp.float32), "rep")
    return finish(
        where,
        packed,
        (backs[:2], backs_other[:2]),
        ((own, backs[2:]), (own_other, backs_other[2:])),
        (own_rows, own_rows_other),
        (far,),
        (from_sub, from_sub_other),
    )


def shards_any(panel_field, near_row, near_col, near_block, bases, far_row, far_col, coupling):
    owner, sub, core = lax.axis_index("clu"), lax.axis_index("sub"), lax.axis_index("rep")
    owners, subs = lax.axis_size("clu"), lax.axis_size("sub")
    where = jnp.stack([owner, sub, core]).astype(jnp.int32)
    clusters, panels, width = panel_field.shape
    packed, _ = pack(where, panel_field, jnp.swapaxes(bases, 1, 2))
    around = lax.all_gather(packed, "sub", axis=0)
    gathered = lax.all_gather(packed, "clu", axis=0, tiled=True)
    slots = owners * clusters
    def slot_of(cluster, owner, core):
        return cluster

    held, matrix = load(slots, far_row, far_col, coupling, near_block)
    back = back_sums(
        slots,
        slot_of,
        [(around[k], lambda o, s, r, k=k: (0, k)) for k in range(subs)],
        where,
        near_row,
        near_col,
        matrix,
        held,
    )
    back = lax.psum(lax.psum_scatter(back, "clu", scatter_dimension=0, tiled=True), "rep")
    ahead, behind, full, held = forward_far(
        slots, [(gathered, lambda o, s, r: (0,) * slots)], where, near_row, near_col, matrix, near_block
    )
    taken = swap(behind, "rep")
    near = forward_own(where, near_row, near_col, held, full, width)
    near = near + swap(near, "rep")
    far = lax.psum((ahead + taken)[(subs - 1) * panels :], "sub").reshape(clusters, -1, width)
    ahead = (ahead + taken)[: (subs - 1) * panels]
    for turn in range(1, subs):
        got = lax.ppermute(
            ahead[(turn - 1) * panels : turn * panels],
            "sub",
            [(s, (s + turn) % subs) for s in range(subs)],
        )
        near = near + jnp.where(core == 0, jnp.stack([got, swap(got, "rep")]), jnp.stack([swap(got, "rep"), got]))
    single = lax.dynamic_slice_in_dim(back, core, 1, axis=0)
    other = lax.dynamic_slice_in_dim(back, 1 - core, 1, axis=0)
    return finish(where, packed, (), ((single,), (other,)), (near,), (far,), ())


def shards(*arrays):
    sizes = tuple(lax.axis_size(axis) for axis in ("clu", "sub", "rep"))
    if sizes == (4, 2, 2):
        return shards_small(*arrays)
    return shards_any(*arrays)


def solution(mesh):
    placed = (
        P(("parts", "clu"), "sub", None),
        P(("parts", "clu", "rep")),
        P(("parts", "clu", "rep")),
        P(("parts", "clu", "rep"), None, "sub"),
        P(("parts", "clu"), "sub", None),
        P(("parts", "clu", "rep")),
        P(("parts", "clu", "rep")),
        P(("parts", "clu", "rep"), None, None),
    )
    return jax.shard_map(
        shards,
        mesh=mesh,
        in_specs=placed,
        out_specs=P(("parts", "clu"), "sub", None),
        check_vma=False,
    )
```

```python
import functools

import jax
import jax.numpy as jnp
from jax import lax
from jax.experimental import pallas as pl
from jax.experimental.pallas import tpu as pltpu
from jax.sharding import PartitionSpec as P

LAST = (((1,), (1,)), ((), ()))
FIRST = (((0,), (0,)), ((), ()))
VMEM = pl.BlockSpec(memory_space=pltpu.VMEM)
ANY = pl.BlockSpec(memory_space=pl.ANY)
ROOM = pltpu.CompilerParams(vmem_limit_bytes=32 * 1024 * 1024)


def in_hbm(array):
    return pltpu.with_memory_space_constraint(array, pltpu.HBM)


PARTS = 4


def place():
    return lax.axis_index("clu"), lax.axis_index("sub"), lax.axis_index("rep")


class Scalars:
    def __init__(self, sources, held, sems):
        self.held = held
        self.copies = [
            pltpu.make_async_copy(source, target, sems.at[k])
            for k, (source, target) in enumerate(zip(sources, held))
        ]
        for copy in self.copies:
            copy.start()

    def wait(self):
        for copy in self.copies:
            copy.wait()
        return self.held


def scalar_scratch(*arrays):
    return [pltpu.SMEM(array.shape, jnp.int32) for array in arrays] + [
        pltpu.SemaphoreType.DMA((len(arrays),))
    ]


def parts_of(block, held, sems):
    pairs = block.shape[0]
    cuts = [pairs * k // PARTS for k in range(PARTS + 1)]
    return [
        (
            range(a, b),
            pltpu.make_async_copy(block.at[pl.ds(a, b - a)], held.at[pl.ds(a, b - a)], sems.at[k]),
        )
        for k, (a, b) in enumerate(zip(cuts, cuts[1:]))
    ]


def load_kernel(far_row, far_col, coupling, block, held, matrix, couplings, table, sems, sem, *scratch):
    parts = parts_of(block, held, sems)
    for _, copy in parts:
        copy.start()
    first = pltpu.make_async_copy(coupling, couplings, sem)
    first.start()
    scalars = Scalars((far_row, far_col), scratch[:2], scratch[2])
    table[...] = jnp.zeros_like(table)
    rows, columns = scalars.wait()
    first.wait()
    sum_couplings(rows, columns, couplings, matrix, table)
    for _, copy in parts:
        copy.wait()


def sum_couplings(far_row, far_col, coupling, matrix, table):
    rank = coupling.shape[1]
    for f in range(coupling.shape[0]):
        at = (far_row[f], far_col[f])
        table[at] = table[at] + coupling[f]
    for c in range(table.shape[0]):
        matrix[c * rank : (c + 1) * rank, :] = jnp.concatenate(
            [table[c, t] for t in range(table.shape[1])], axis=1
        )


def load(slots, far_row, far_col, coupling, block):
    rank = coupling.shape[1]
    return pl.pallas_call(
        load_kernel,
        out_shape=(
            jax.ShapeDtypeStruct(block.shape, block.dtype),
            jax.ShapeDtypeStruct((2 * rank, slots * rank), jnp.float32),
        ),
        in_specs=[ANY] * 4,
        out_specs=(VMEM, VMEM),
        scratch_shapes=[
            pltpu.VMEM(coupling.shape, coupling.dtype),
            pltpu.VMEM((2, slots, rank, rank), jnp.float32),
            pltpu.SemaphoreType.DMA((PARTS,)),
            pltpu.SemaphoreType.DMA,
            *scalar_scratch(far_row, far_col),
        ],
        compiler_params=ROOM,
    )(in_hbm(far_row), in_hbm(far_col), in_hbm(coupling), in_hbm(block))


def pack_kernel(panel, bases, packed, mine, held, sems):
    clusters, _, width = panel.shape
    moves = []
    for c in range(clusters):
        moves.append(pltpu.make_async_copy(panel.at[c], held.at[c], sems.at[2 * c]))
        moves.append(
            pltpu.make_async_copy(bases.at[c], packed.at[c, pl.ds(width, bases.shape[1])], sems.at[2 * c + 1])
        )
    for move in moves:
        move.start()
    for c in range(clusters):
        moves[2 * c].wait()
        packed[c, :width, :] = held[c].T
    for c in range(clusters):
        moves[2 * c + 1].wait()
    mine[0] = packed[place()[2]]


def pack(panel, bases):
    clusters, panels, width = panel.shape
    rows = width + bases.shape[1]
    return pl.pallas_call(
        pack_kernel,
        out_shape=(
            jax.ShapeDtypeStruct((clusters, rows, panels), panel.dtype),
            jax.ShapeDtypeStruct((1, rows, panels), panel.dtype),
        ),
        in_specs=[ANY, ANY],
        out_specs=(VMEM, VMEM),
        scratch_shapes=[
            pltpu.VMEM(panel.shape, panel.dtype),
            pltpu.SemaphoreType.DMA((2 * clusters,)),
        ],
        compiler_params=ROOM,
    )(in_hbm(panel), in_hbm(bases))


def parts_in_bfloat16(value, count):
    out = []
    for _ in range(count):
        out.append(value.astype(jnp.bfloat16))
        value = value - out[-1].astype(jnp.float32)
    return out


def product_in_parts(left, right, dims):
    (inner_left,), (inner_right,) = dims[0]
    left_high, left_low = parts_in_bfloat16(left, 2)
    right_high, right_low = parts_in_bfloat16(right, 2)
    return lax.dot_general(
        jnp.concatenate([left_high, left_high, left_low], axis=inner_left),
        jnp.concatenate([right_high, right_low, right_high], axis=inner_right),
        dims,
        preferred_element_type=jnp.float32,
    )


def each_pair(pairs, step):
    for q in range(pairs):
        step(q)


def back_kernel(plan, slot_of, near_row, near_col, matrix, block, *refs):
    n = len(plan)
    pieces = refs[:n]
    total, full, *scratch = refs[n:]
    scalars = Scalars((near_row, near_col), scratch[:2], scratch[2])
    panels = block.shape[2]
    clusters, rows = full.shape[:2]
    rank = matrix.shape[0] // clusters
    width = rows - rank
    total[:, :width, :] = jnp.zeros((total.shape[0], width, panels), jnp.float32)
    index = place()
    near_row, near_col = scalars.wait()
    for piece, where in zip(pieces, plan):
        first, sub = where(index[0], index[1], index[2])
        for c in range(piece.shape[0]):
            full[first + c, :, pl.ds(pl.multiple_of(sub * panels, panels), panels)] = piece[c]
    projection = jnp.concatenate(
        [
            lax.dot_general(
                full[c, width:, :], full[c, :width, :], LAST, preferred_element_type=jnp.float32
            )
            for c in range(clusters)
        ],
        axis=0,
    )
    weights = product_in_parts(matrix[...], projection, FIRST)
    for t in range(total.shape[0]):
        slot = slot_of(t, index[0], index[2])
        for i in range(width // panels):
            total[slot, width + i * rank : width + (i + 1) * rank, :] = weights[
                t * rank : (t + 1) * rank, i * panels : (i + 1) * panels
            ]

    def step(q):
        product = jnp.dot(
            full[near_row[q], :width, :], block[q], preferred_element_type=jnp.float32
        )
        slot = slot_of(near_col[q], index[0], index[2])
        total[slot, :width, :] += product.astype(jnp.bfloat16).astype(jnp.float32)

    each_pair(block.shape[0], step)


def back_sums(slots, slot_of, pieces, near_row, near_col, matrix, block):
    rows = pieces[0][0].shape[1]
    _, full_panels, panels = block.shape
    rank = matrix.shape[1] // slots
    width = rows - rank
    tall = width + rank * (width // panels)
    plan = tuple(where for _, where in pieces)
    return pl.pallas_call(
        functools.partial(back_kernel, plan, slot_of),
        out_shape=jax.ShapeDtypeStruct((slots, tall, panels), jnp.float32),
        in_specs=[ANY] * 2 + [VMEM] * (2 + len(pieces)),
        out_specs=VMEM,
        scratch_shapes=[
            pltpu.VMEM((2, rows, full_panels), jnp.bfloat16),
            *scalar_scratch(near_row, near_col),
        ],
        compiler_params=ROOM,
    )(in_hbm(near_row), in_hbm(near_col), matrix, block, *[p for p, _ in pieces])


def forward_step(turns, index, near_row, near_col, block, full, total):
    rows, panels = total.shape[1] // len(turns), block.shape[2]
    subs = block.shape[1] // panels

    def step(q):
        field = full[near_col[q], : total.shape[2], :]
        row = near_row[q]
        for k, turn in enumerate(turns):
            at = lax.rem(index[1] + turn, subs)
            product = lax.dot_general(
                block[q, pl.ds(pl.multiple_of(at * panels, panels), panels), :],
                field,
                LAST,
                preferred_element_type=jnp.float32,
            )
            total[row, k * rows : (k + 1) * rows, :] += product

    return step


def forward_kernel(plan, turns, near_row, near_col, matrix, block, *refs):
    n = len(plan)
    pieces = refs[:n]
    keep, give, full, held, total, sems, *scratch = refs[n:]
    scalars = Scalars((near_row, near_col), scratch[:2], scratch[2])
    parts = parts_of(block, held, sems)
    for _, copy in parts:
        copy.start()
    slots, rows, _ = full.shape
    rank = matrix.shape[1] // slots
    width = rows - rank
    total[...] = jnp.zeros_like(total)
    index = place()
    near_row, near_col = scalars.wait()
    for piece, where in zip(pieces, plan):
        firsts = where(index[0], index[1], index[2])
        for c, first in enumerate(firsts):
            full[first + c] = piece[c]
    projection = jnp.concatenate(
        [
            lax.dot_general(
                full[t, width:, :], full[t, :width, :], LAST, preferred_element_type=jnp.float32
            )
            for t in range(slots)
        ],
        axis=0,
    )
    weights = product_in_parts(matrix[...], projection, (((1,), (0,)), ((), ())))
    step = forward_step(turns, index, near_row, near_col, held, full, total)
    for pairs, copy in parts:
        copy.wait()
        for q in pairs:
            step(q)
    core, tall = index[2], total.shape[1]
    keep[:tall, :] = total[core]
    keep[tall:, :] = weights
    give[:tall, :] = total[1 - core]
    give[tall:, :] = weights


def forward_far(slots, pieces, near_row, near_col, matrix, block):
    rows = pieces[0][0].shape[1]
    _, full_panels, panels = block.shape
    rank = matrix.shape[1] // slots
    width = rows - rank
    plan = tuple(where for _, where in pieces)
    turns = tuple(range(1, full_panels // panels))
    tall = panels * len(turns)
    shape = jax.ShapeDtypeStruct((tall + 2 * rank, width), jnp.float32)
    return pl.pallas_call(
        functools.partial(forward_kernel, plan, turns),
        out_shape=(
            shape,
            shape,
            jax.ShapeDtypeStruct((slots, rows, panels), jnp.bfloat16),
            jax.ShapeDtypeStruct(block.shape, block.dtype),
        ),
        in_specs=[ANY] * 2 + [VMEM, ANY] + [VMEM] * len(pieces),
        out_specs=(VMEM,) * 4,
        scratch_shapes=[
            pltpu.VMEM((2, tall, width), jnp.float32),
            pltpu.SemaphoreType.DMA((PARTS,)),
            *scalar_scratch(near_row, near_col),
        ],
        compiler_params=ROOM,
    )(in_hbm(near_row), in_hbm(near_col), matrix, in_hbm(block), *[p for p, _ in pieces])


def merge_kernel(keep, taken, payload, far):
    rank = far.shape[1]
    panels = keep.shape[0] - 2 * rank
    core = place()[2]
    for c in range(2):
        rows = slice(panels + c * rank, panels + (c + 1) * rank)
        far[c] = keep[rows, :] + taken[rows, :]
    weights = far[core]
    high = weights.astype(payload.dtype)
    payload[:panels, :] = (keep[:panels] + taken[:panels]).astype(payload.dtype)
    payload[panels : panels + rank, :] = high
    payload[panels + rank :, :] = (weights - high.astype(jnp.float32)).astype(payload.dtype)


def to_other_sub(keep, taken, panels):
    rows, width = keep.shape
    rank = (rows - panels) // 2
    return pl.pallas_call(
        merge_kernel,
        out_shape=(
            jax.ShapeDtypeStruct((rows, width), jnp.bfloat16),
            jax.ShapeDtypeStruct((2, rank, width), jnp.float32),
        ),
        in_specs=[VMEM, VMEM],
        out_specs=(VMEM, VMEM),
        compiler_params=ROOM,
    )(keep, taken)


def own_kernel(near_row, near_col, block, full, total, *scratch):
    scalars = Scalars((near_row, near_col), scratch[:2], scratch[2])
    total[...] = jnp.zeros_like(total)
    index = place()
    near_row, near_col = scalars.wait()
    each_pair(
        block.shape[0], forward_step((0,), index, near_row, near_col, block, full, total)
    )


def forward_own(near_row, near_col, block, full, width):
    return pl.pallas_call(
        own_kernel,
        out_shape=jax.ShapeDtypeStruct((2, block.shape[2], width), jnp.float32),
        in_specs=[ANY] * 2 + [VMEM, VMEM],
        out_specs=VMEM,
        scratch_shapes=scalar_scratch(near_row, near_col),
        compiler_params=ROOM,
    )(in_hbm(near_row), in_hbm(near_col), block, full)


def finish_kernel(counts, packed, *refs):
    refs = list(refs)
    both, backs, nears, fars, subs = ([refs.pop(0) for _ in range(count)] for count in counts)
    result, back, weight = refs
    core = place()[2]
    clusters, rows, panels = packed.shape
    width = result.shape[2]
    rank = rows - width
    half = len(backs) // 2
    for k, at in enumerate((core, 1 - core)):
        back[at] = sum(
            term[0].astype(jnp.float32) for term in backs[k * half : (k + 1) * half]
        )
        near = sum(term[at] for term in nears)
        far = sum(term[at] for term in fars)
        if subs:
            got = subs[k]
            near += got[:panels].astype(jnp.float32)
            far += got[panels : panels + rank].astype(jnp.float32)
            far += got[panels + rank :].astype(jnp.float32)
        result[at] = near
        weight[at] = far
    for term in both:
        back[...] += term[...].astype(jnp.float32)
    for c in range(clusters):
        for i in range(width // panels):
            weight[c, :, i * panels : (i + 1) * panels] += back[
                c, width + i * rank : width + (i + 1) * rank, :
            ]
        result[c] += back[c, :width, :].T + lax.dot_general(
            jnp.concatenate([packed[c, width:, :]] * 3, axis=0),
            jnp.concatenate(parts_in_bfloat16(weight[c], 3), axis=0),
            FIRST,
            preferred_element_type=jnp.float32,
        )


def finish(packed, both, backs, nears, fars, subs):
    groups = (both, backs[0] + backs[1], nears, fars, subs)
    return pl.pallas_call(
        functools.partial(finish_kernel, tuple(len(group) for group in groups)),
        out_shape=jax.ShapeDtypeStruct(nears[0].shape, jnp.float32),
        in_specs=[VMEM] * (1 + sum(len(group) for group in groups)),
        out_specs=VMEM,
        scratch_shapes=[
            pltpu.VMEM((packed.shape[0],) + backs[0][0].shape[1:], jnp.float32),
            pltpu.VMEM(fars[0].shape, jnp.float32),
        ],
        compiler_params=ROOM,
    )(packed, *[array for group in groups for array in group])


def swap(value, axis):
    return lax.ppermute(value, axis, [(0, 1), (1, 0)])


def stage(apart, run, *operands):
    shapes = jax.eval_shape(run, *operands)
    return lax.cond(
        apart,
        run,
        lambda *_: jax.tree.map(lambda v: jnp.zeros(v.shape, v.dtype), shapes),
        *operands,
    )


def shards_small(panel_field, near_row, near_col, near_block, bases, far_row, far_col, coupling):
    owner, sub, core = lax.axis_index("clu"), lax.axis_index("sub"), lax.axis_index("rep")
    _, panels, width = panel_field.shape
    rank = bases.shape[2]
    packed, mine = pack(panel_field, jnp.swapaxes(bases, 1, 2))

    axes = ("clu", "sub", "rep")
    numbered = [(o, s, r) for o in range(4) for s in range(2) for r in range(2)]
    by_core = [(i, ((o ^ (1 + r)) * 2 + s) * 2 + r) for i, (o, s, r) in enumerate(numbered)]
    opposite = [(o, o ^ 3) for o in range(4)]

    across = swap(mine, "sub")
    incoming = [lax.ppermute(packed[c : c + 1], axes, by_core) for c in range(2)]
    incoming.append(lax.ppermute(mine, "clu", opposite))
    held = near_block

    def slot_of(cluster, owner, core):
        turn = lax.shift_right_logical(cluster, 1) ^ owner
        local = cluster & 1
        paired = (turn == 1) | (turn == 2)
        kept = jnp.where(paired, turn == 1 + core, local == core)
        within = jnp.where(paired, local, jnp.where(turn == 3, 2, 3))
        return jnp.where(kept, within, 4 + within)

    apart = owner >= 0

    def back_half(packed, across, near_row, near_col, far_row, far_col, coupling, block):
        across_other = swap(across, "rep")
        held, matrix = load(8, far_row, far_col, coupling, block)
        total = back_sums(
            8,
            slot_of,
            [
                (packed, lambda o, s, r: (0, s)),
                (across, lambda o, s, r: (r, 1 - s)),
                (across_other, lambda o, s, r: (1 - r, 1 - s)),
            ],
            near_row,
            near_col,
            matrix,
            held,
        )
        taken = swap(total[4:], "rep")
        to_two = (total[:2] + taken[:2]).astype(jnp.bfloat16)
        to_one = (total[2:3] + taken[2:3]).astype(jnp.bfloat16)
        return to_two, to_one, total[3:4] + taken[3:], matrix

    to_two, to_one, own, matrix = stage(
        apart,
        back_half,
        packed,
        across,
        near_row,
        near_col,
        far_row,
        far_col,
        coupling,
        near_block,
    )
    first, second, third = incoming
    to_one, third = lax.optimization_barrier((to_one, third))
    to_two, first, third = lax.optimization_barrier((to_two, first, third))
    to_two, *incoming = lax.optimization_barrier((to_two, first, second, third))
    back_two = lax.ppermute(to_two, axes, by_core)
    back_one = lax.ppermute(to_one, "clu", opposite)
    incoming = jnp.concatenate(incoming, axis=0)
    incoming_other = swap(incoming, "rep")

    def forward_half(packed, incoming, incoming_other, matrix, near_row, near_col, block):
        ahead, behind, full, held = forward_far(
            8,
            [
                (packed, lambda o, s, r: (2 * o,) * 2),
                (incoming, lambda o, s, r: (2 * (o ^ (1 + r)),) * 2 + (2 * (o ^ 3) + r - 2,)),
                (
                    incoming_other,
                    lambda o, s, r: (2 * (o ^ (2 - r)),) * 2 + (2 * (o ^ 3) + 1 - r - 2,),
                ),
            ],
            near_row,
            near_col,
            matrix,
            block,
        )
        own_rows = forward_own(near_row, near_col, held, full, width)
        payload, far = to_other_sub(ahead, swap(behind, "rep"), panels)
        return payload, far, own_rows

    payload, far, own_rows = stage(
        apart,
        forward_half,
        packed,
        incoming,
        incoming_other,
        matrix,
        near_row,
        near_col,
        near_block,
    )

    from_sub = swap(payload, "sub")
    backs = jnp.concatenate([back_two, back_one], axis=0)
    backs_other = swap(backs, "rep")
    own_other, own_rows_other = swap(own, "rep"), swap(own_rows, "rep")
    own_other, from_sub = lax.optimization_barrier((own_other, from_sub))
    from_sub_other = swap(from_sub.astype(jnp.float32), "rep")
    return finish(
        packed,
        (backs[:2], backs_other[:2]),
        ((own, backs[2:]), (own_other, backs_other[2:])),
        (own_rows, own_rows_other),
        (far,),
        (from_sub, from_sub_other),
    )


def shards_any(panel_field, near_row, near_col, near_block, bases, far_row, far_col, coupling):
    owner, sub, core = lax.axis_index("clu"), lax.axis_index("sub"), lax.axis_index("rep")
    owners, subs = lax.axis_size("clu"), lax.axis_size("sub")
    clusters, panels, width = panel_field.shape
    packed, _ = pack(panel_field, jnp.swapaxes(bases, 1, 2))
    around = lax.all_gather(packed, "sub", axis=0)
    gathered = lax.all_gather(packed, "clu", axis=0, tiled=True)
    slots = owners * clusters
    def slot_of(cluster, owner, core):
        return cluster

    held, matrix = load(slots, far_row, far_col, coupling, near_block)
    back = back_sums(
        slots,
        slot_of,
        [(around[k], lambda o, s, r, k=k: (0, k)) for k in range(subs)],
        near_row,
        near_col,
        matrix,
        held,
    )
    back = lax.psum(lax.psum_scatter(back, "clu", scatter_dimension=0, tiled=True), "rep")
    ahead, behind, full, held = forward_far(
        slots, [(gathered, lambda o, s, r: (0,) * slots)], near_row, near_col, matrix, near_block
    )
    taken = swap(behind, "rep")
    near = forward_own(near_row, near_col, held, full, width)
    near = near + swap(near, "rep")
    far = lax.psum((ahead + taken)[(subs - 1) * panels :], "sub").reshape(clusters, -1, width)
    ahead = (ahead + taken)[: (subs - 1) * panels]
    for turn in range(1, subs):
        got = lax.ppermute(
            ahead[(turn - 1) * panels : turn * panels],
            "sub",
            [(s, (s + turn) % subs) for s in range(subs)],
        )
        near = near + jnp.where(core == 0, jnp.stack([got, swap(got, "rep")]), jnp.stack([swap(got, "rep"), got]))
    single = lax.dynamic_slice_in_dim(back, core, 1, axis=0)
    other = lax.dynamic_slice_in_dim(back, 1 - core, 1, axis=0)
    return finish(packed, (), ((single,), (other,)), (near,), (far,), ())


def shards(*arrays):
    sizes = tuple(lax.axis_size(axis) for axis in ("clu", "sub", "rep"))
    if sizes == (4, 2, 2):
        return shards_small(*arrays)
    return shards_any(*arrays)


def solution(mesh):
    placed = (
        P(("parts", "clu"), "sub", None),
        P(("parts", "clu", "rep")),
        P(("parts", "clu", "rep")),
        P(("parts", "clu", "rep"), None, "sub"),
        P(("parts", "clu"), "sub", None),
        P(("parts", "clu", "rep")),
        P(("parts", "clu", "rep")),
        P(("parts", "clu", "rep"), None, None),
    )
    return jax.shard_map(
        shards,
        mesh=mesh,
        in_specs=placed,
        out_specs=P(("parts", "clu"), "sub", None),
        check_vma=False,
    )
```

```python
import functools

import jax
import jax.numpy as jnp
from jax import lax
from jax.experimental import pallas as pl
from jax.experimental.pallas import tpu as pltpu
from jax.sharding import PartitionSpec as P

LAST = (((1,), (1,)), ((), ()))
FIRST = (((0,), (0,)), ((), ()))
VMEM = pl.BlockSpec(memory_space=pltpu.VMEM)
ANY = pl.BlockSpec(memory_space=pl.ANY)
ROOM = pltpu.CompilerParams(vmem_limit_bytes=32 * 1024 * 1024)


def in_hbm(array):
    return pltpu.with_memory_space_constraint(array, pltpu.HBM)


PARTS = 4


def place():
    return lax.axis_index("clu"), lax.axis_index("sub"), lax.axis_index("rep")


class Scalars:
    def __init__(self, sources, held, sems):
        self.held = held
        self.copies = [
            pltpu.make_async_copy(source, target, sems.at[k])
            for k, (source, target) in enumerate(zip(sources, held))
        ]
        for copy in self.copies:
            copy.start()

    def wait(self):
        for copy in self.copies:
            copy.wait()
        return self.held


def scalar_scratch(*arrays):
    return [pltpu.SMEM(array.shape, jnp.int32) for array in arrays] + [
        pltpu.SemaphoreType.DMA((len(arrays),))
    ]


def parts_of(block, held, sems):
    pairs = block.shape[0]
    cuts = [pairs * k // PARTS for k in range(PARTS + 1)]
    return [
        (
            range(a, b),
            pltpu.make_async_copy(block.at[pl.ds(a, b - a)], held.at[pl.ds(a, b - a)], sems.at[k]),
        )
        for k, (a, b) in enumerate(zip(cuts, cuts[1:]))
    ]


def load_kernel(
    near_row, near_col, far_row, far_col, coupling, block,
    held, matrix, row_held, col_held, couplings, table, sems, sem, *scratch
):
    scalars = Scalars((far_row, far_col), scratch[:2], scratch[2])
    small = Scalars((near_row, near_col), (row_held, col_held), scratch[3])
    first = pltpu.make_async_copy(coupling, couplings, sem)
    first.start()
    parts = parts_of(block, held, sems)
    for _, copy in parts:
        copy.start()
    table[...] = jnp.zeros_like(table)
    rows, columns = scalars.wait()
    first.wait()
    sum_couplings(rows, columns, couplings, matrix, table)
    small.wait()
    for _, copy in parts:
        copy.wait()


def sum_couplings(far_row, far_col, coupling, matrix, table):
    rank = coupling.shape[1]
    for f in range(coupling.shape[0]):
        at = (far_row[f], far_col[f])
        table[at] = table[at] + coupling[f]
    for c in range(table.shape[0]):
        matrix[c * rank : (c + 1) * rank, :] = jnp.concatenate(
            [table[c, t] for t in range(table.shape[1])], axis=1
        )


def load(slots, near_row, near_col, far_row, far_col, coupling, block):
    rank = coupling.shape[1]
    return pl.pallas_call(
        load_kernel,
        out_shape=(
            jax.ShapeDtypeStruct(block.shape, block.dtype),
            jax.ShapeDtypeStruct((2 * rank, slots * rank), jnp.float32),
            jax.ShapeDtypeStruct(near_row.shape, jnp.int32),
            jax.ShapeDtypeStruct(near_col.shape, jnp.int32),
        ),
        in_specs=[ANY] * 6,
        out_specs=(VMEM,) * 4,
        scratch_shapes=[
            pltpu.VMEM(coupling.shape, coupling.dtype),
            pltpu.VMEM((2, slots, rank, rank), jnp.float32),
            pltpu.SemaphoreType.DMA((PARTS,)),
            pltpu.SemaphoreType.DMA,
            *scalar_scratch(far_row, far_col),
            pltpu.SemaphoreType.DMA((2,)),
        ],
        compiler_params=ROOM,
    )(*[in_hbm(array) for array in (near_row, near_col, far_row, far_col, coupling, block)])


def pack_kernel(panel, bases, packed, mine, held, sems):
    clusters, _, width = panel.shape
    moves = []
    for c in range(clusters):
        moves.append(pltpu.make_async_copy(panel.at[c], held.at[c], sems.at[2 * c]))
        moves.append(
            pltpu.make_async_copy(bases.at[c], packed.at[c, pl.ds(width, bases.shape[1])], sems.at[2 * c + 1])
        )
    for move in moves:
        move.start()
    for c in range(clusters):
        moves[2 * c].wait()
        packed[c, :width, :] = held[c].T
    for c in range(clusters):
        moves[2 * c + 1].wait()
    mine[0] = packed[place()[2]]


def pack(panel, bases):
    clusters, panels, width = panel.shape
    rows = width + bases.shape[1]
    return pl.pallas_call(
        pack_kernel,
        out_shape=(
            jax.ShapeDtypeStruct((clusters, rows, panels), panel.dtype),
            jax.ShapeDtypeStruct((1, rows, panels), panel.dtype),
        ),
        in_specs=[ANY, ANY],
        out_specs=(VMEM, VMEM),
        scratch_shapes=[
            pltpu.VMEM(panel.shape, panel.dtype),
            pltpu.SemaphoreType.DMA((2 * clusters,)),
        ],
        compiler_params=ROOM,
    )(in_hbm(panel), in_hbm(bases))


def parts_in_bfloat16(value, count):
    out = []
    for _ in range(count):
        out.append(value.astype(jnp.bfloat16))
        value = value - out[-1].astype(jnp.float32)
    return out


def product_in_parts(left, right, dims):
    (inner_left,), (inner_right,) = dims[0]
    left_high, left_low = parts_in_bfloat16(left, 2)
    right_high, right_low = parts_in_bfloat16(right, 2)
    return lax.dot_general(
        jnp.concatenate([left_high, left_high, left_low], axis=inner_left),
        jnp.concatenate([right_high, right_low, right_high], axis=inner_right),
        dims,
        preferred_element_type=jnp.float32,
    )


def each_pair(pairs, step):
    for q in range(pairs):
        step(q)


def back_kernel(plan, slot_of, near_row, near_col, matrix, block, *refs):
    n = len(plan)
    pieces = refs[:n]
    total, full, *scratch = refs[n:]
    scalars = Scalars((near_row, near_col), scratch[:2], scratch[2])
    panels = block.shape[2]
    clusters, rows = full.shape[:2]
    rank = matrix.shape[0] // clusters
    width = rows - rank
    total[:, :width, :] = jnp.zeros((total.shape[0], width, panels), jnp.float32)
    index = place()
    near_row, near_col = scalars.wait()
    for piece, where in zip(pieces, plan):
        first, sub = where(index[0], index[1], index[2])
        for c in range(piece.shape[0]):
            full[first + c, :, pl.ds(pl.multiple_of(sub * panels, panels), panels)] = piece[c]
    projection = jnp.concatenate(
        [
            lax.dot_general(
                full[c, width:, :], full[c, :width, :], LAST, preferred_element_type=jnp.float32
            )
            for c in range(clusters)
        ],
        axis=0,
    )
    weights = product_in_parts(matrix[...], projection, FIRST)
    for t in range(total.shape[0]):
        slot = slot_of(t, index[0], index[2])
        for i in range(width // panels):
            total[slot, width + i * rank : width + (i + 1) * rank, :] = weights[
                t * rank : (t + 1) * rank, i * panels : (i + 1) * panels
            ]

    def step(q):
        product = jnp.dot(
            full[near_row[q], :width, :], block[q], preferred_element_type=jnp.float32
        )
        slot = slot_of(near_col[q], index[0], index[2])
        total[slot, :width, :] += product.astype(jnp.bfloat16).astype(jnp.float32)

    each_pair(block.shape[0], step)


def back_sums(slots, slot_of, pieces, near_row, near_col, matrix, block):
    rows = pieces[0][0].shape[1]
    _, full_panels, panels = block.shape
    rank = matrix.shape[1] // slots
    width = rows - rank
    tall = width + rank * (width // panels)
    plan = tuple(where for _, where in pieces)
    return pl.pallas_call(
        functools.partial(back_kernel, plan, slot_of),
        out_shape=jax.ShapeDtypeStruct((slots, tall, panels), jnp.float32),
        in_specs=[ANY] * 2 + [VMEM] * (2 + len(pieces)),
        out_specs=VMEM,
        scratch_shapes=[
            pltpu.VMEM((2, rows, full_panels), jnp.bfloat16),
            *scalar_scratch(near_row, near_col),
        ],
        compiler_params=ROOM,
    )(near_row, near_col, matrix, block, *[p for p, _ in pieces])


def forward_step(turns, index, near_row, near_col, block, full, total):
    rows, panels = total.shape[1] // len(turns), block.shape[2]
    subs = block.shape[1] // panels

    def step(q):
        field = full[near_col[q]]
        row = near_row[q]
        for k, turn in enumerate(turns):
            at = lax.rem(index[1] + turn, subs)
            product = jnp.dot(
                block[q, pl.ds(pl.multiple_of(at * panels, panels), panels), :],
                field,
                preferred_element_type=jnp.float32,
            )
            total[row, k * rows : (k + 1) * rows, :] += product

    return step


def forward_kernel(plan, turns, near_row, near_col, matrix, block, *refs):
    n = len(plan)
    pieces = refs[:n]
    keep, give, full, held, total, projection, sems, *scratch = refs[n:]
    scalars = Scalars((near_row, near_col), scratch[:2], scratch[2])
    parts = parts_of(block, held, sems)
    for _, copy in parts:
        copy.start()
    slots, _, width = full.shape
    rank = matrix.shape[1] // slots
    total[...] = jnp.zeros_like(total)
    index = place()
    near_row, near_col = scalars.wait()
    for piece, where in zip(pieces, plan):
        firsts = where(index[0], index[1], index[2])
        for c, first in enumerate(firsts):
            panel = piece[c, :width, :].T
            full[first + c] = panel
            projection[pl.ds(pl.multiple_of((first + c) * rank, rank), rank), :] = jnp.dot(
                piece[c, width:, :], panel, preferred_element_type=jnp.float32
            )
    weights = product_in_parts(matrix[...], projection[...], (((1,), (0,)), ((), ())))
    step = forward_step(turns, index, near_row, near_col, held, full, total)
    for pairs, copy in parts:
        copy.wait()
        for q in pairs:
            step(q)
    core, tall = index[2], total.shape[1]
    keep[:tall, :] = total[core]
    keep[tall:, :] = weights
    give[:tall, :] = total[1 - core]
    give[tall:, :] = weights


def forward_far(slots, pieces, near_row, near_col, matrix, block):
    rows = pieces[0][0].shape[1]
    _, full_panels, panels = block.shape
    rank = matrix.shape[1] // slots
    width = rows - rank
    plan = tuple(where for _, where in pieces)
    turns = tuple(range(1, full_panels // panels))
    tall = panels * len(turns)
    shape = jax.ShapeDtypeStruct((tall + 2 * rank, width), jnp.float32)
    return pl.pallas_call(
        functools.partial(forward_kernel, plan, turns),
        out_shape=(
            shape,
            shape,
            jax.ShapeDtypeStruct((slots, panels, width), jnp.bfloat16),
            jax.ShapeDtypeStruct(block.shape, block.dtype),
        ),
        in_specs=[ANY] * 2 + [VMEM, ANY] + [VMEM] * len(pieces),
        out_specs=(VMEM,) * 4,
        scratch_shapes=[
            pltpu.VMEM((2, tall, width), jnp.float32),
            pltpu.VMEM((slots * rank, width), jnp.float32),
            pltpu.SemaphoreType.DMA((PARTS,)),
            *scalar_scratch(near_row, near_col),
        ],
        compiler_params=ROOM,
    )(in_hbm(near_row), in_hbm(near_col), matrix, in_hbm(block), *[p for p, _ in pieces])


def merge_kernel(keep, taken, payload, far):
    rank = far.shape[1]
    panels = keep.shape[0] - 2 * rank
    core = place()[2]
    for c in range(2):
        rows = slice(panels + c * rank, panels + (c + 1) * rank)
        far[c] = keep[rows, :] + taken[rows, :]
    weights = far[core]
    high = weights.astype(payload.dtype)
    payload[:panels, :] = (keep[:panels] + taken[:panels]).astype(payload.dtype)
    payload[panels : panels + rank, :] = high
    payload[panels + rank :, :] = (weights - high.astype(jnp.float32)).astype(payload.dtype)


def to_other_sub(keep, taken, panels):
    rows, width = keep.shape
    rank = (rows - panels) // 2
    return pl.pallas_call(
        merge_kernel,
        out_shape=(
            jax.ShapeDtypeStruct((rows, width), jnp.bfloat16),
            jax.ShapeDtypeStruct((2, rank, width), jnp.float32),
        ),
        in_specs=[VMEM, VMEM],
        out_specs=(VMEM, VMEM),
        compiler_params=ROOM,
    )(keep, taken)


def own_kernel(near_row, near_col, block, full, total, *scratch):
    scalars = Scalars((near_row, near_col), scratch[:2], scratch[2])
    total[...] = jnp.zeros_like(total)
    index = place()
    near_row, near_col = scalars.wait()
    each_pair(
        block.shape[0], forward_step((0,), index, near_row, near_col, block, full, total)
    )


def forward_own(near_row, near_col, block, full, width):
    return pl.pallas_call(
        own_kernel,
        out_shape=jax.ShapeDtypeStruct((2, block.shape[2], width), jnp.float32),
        in_specs=[ANY] * 2 + [VMEM, VMEM],
        out_specs=VMEM,
        scratch_shapes=scalar_scratch(near_row, near_col),
        compiler_params=ROOM,
    )(near_row, near_col, block, full)


def finish_kernel(counts, packed, *refs):
    refs = list(refs)
    both, backs, nears, fars, subs = ([refs.pop(0) for _ in range(count)] for count in counts)
    result, back, weight = refs
    core = place()[2]
    clusters, rows, panels = packed.shape
    width = result.shape[2]
    rank = rows - width
    half = len(backs) // 2
    for k, at in enumerate((core, 1 - core)):
        back[at] = sum(
            term[0].astype(jnp.float32) for term in backs[k * half : (k + 1) * half]
        )
        near = sum(term[at] for term in nears)
        far = sum(term[at] for term in fars)
        if subs:
            got = subs[k]
            near += got[:panels].astype(jnp.float32)
            far += got[panels : panels + rank].astype(jnp.float32)
            far += got[panels + rank :].astype(jnp.float32)
        result[at] = near
        weight[at] = far
    for term in both:
        back[...] += term[...].astype(jnp.float32)
    for c in range(clusters):
        for i in range(width // panels):
            weight[c, :, i * panels : (i + 1) * panels] += back[
                c, width + i * rank : width + (i + 1) * rank, :
            ]
        result[c] += back[c, :width, :].T + lax.dot_general(
            jnp.concatenate([packed[c, width:, :]] * 3, axis=0),
            jnp.concatenate(parts_in_bfloat16(weight[c], 3), axis=0),
            FIRST,
            preferred_element_type=jnp.float32,
        )


def finish(packed, both, backs, nears, fars, subs):
    groups = (both, backs[0] + backs[1], nears, fars, subs)
    return pl.pallas_call(
        functools.partial(finish_kernel, tuple(len(group) for group in groups)),
        out_shape=jax.ShapeDtypeStruct(nears[0].shape, jnp.float32),
        in_specs=[VMEM] * (1 + sum(len(group) for group in groups)),
        out_specs=VMEM,
        scratch_shapes=[
            pltpu.VMEM((packed.shape[0],) + backs[0][0].shape[1:], jnp.float32),
            pltpu.VMEM(fars[0].shape, jnp.float32),
        ],
        compiler_params=ROOM,
    )(packed, *[array for group in groups for array in group])


def swap(value, axis):
    return lax.ppermute(value, axis, [(0, 1), (1, 0)])


def stage(apart, run, *operands):
    shapes = jax.eval_shape(run, *operands)
    return lax.cond(
        apart,
        run,
        lambda *_: jax.tree.map(lambda v: jnp.zeros(v.shape, v.dtype), shapes),
        *operands,
    )


def shards_small(panel_field, near_row, near_col, near_block, bases, far_row, far_col, coupling):
    owner, sub, core = lax.axis_index("clu"), lax.axis_index("sub"), lax.axis_index("rep")
    _, panels, width = panel_field.shape
    rank = bases.shape[2]
    packed, mine = pack(panel_field, jnp.swapaxes(bases, 1, 2))

    axes = ("clu", "sub", "rep")
    numbered = [(o, s, r) for o in range(4) for s in range(2) for r in range(2)]
    by_core = [(i, ((o ^ (1 + r)) * 2 + s) * 2 + r) for i, (o, s, r) in enumerate(numbered)]
    opposite = [(o, o ^ 3) for o in range(4)]

    across = swap(mine, "sub")
    incoming = [lax.ppermute(packed[c : c + 1], axes, by_core) for c in range(2)]
    incoming.append(lax.ppermute(mine, "clu", opposite))
    held = near_block

    def slot_of(cluster, owner, core):
        turn = lax.shift_right_logical(cluster, 1) ^ owner
        local = cluster & 1
        paired = (turn == 1) | (turn == 2)
        kept = jnp.where(paired, turn == 1 + core, local == core)
        within = jnp.where(paired, local, jnp.where(turn == 3, 2, 3))
        return jnp.where(kept, within, 4 + within)

    apart = owner >= 0

    def back_half(packed, across, near_row, near_col, far_row, far_col, coupling, block):
        across_other = swap(across, "rep")
        held, matrix, near_row, near_col = load(
            8, near_row, near_col, far_row, far_col, coupling, block
        )
        total = back_sums(
            8,
            slot_of,
            [
                (packed, lambda o, s, r: (0, s)),
                (across, lambda o, s, r: (r, 1 - s)),
                (across_other, lambda o, s, r: (1 - r, 1 - s)),
            ],
            near_row,
            near_col,
            matrix,
            held,
        )
        taken = swap(total[4:], "rep")
        to_two = (total[:2] + taken[:2]).astype(jnp.bfloat16)
        to_one = (total[2:3] + taken[2:3]).astype(jnp.bfloat16)
        return to_two, to_one, total[3:4] + taken[3:], matrix, near_row, near_col

    to_two, to_one, own, matrix, row_held, col_held = stage(
        apart,
        back_half,
        packed,
        across,
        near_row,
        near_col,
        far_row,
        far_col,
        coupling,
        near_block,
    )
    first, second, third = incoming
    to_one, third = lax.optimization_barrier((to_one, third))
    to_two, first, third = lax.optimization_barrier((to_two, first, third))
    to_two, *incoming = lax.optimization_barrier((to_two, first, second, third))
    back_two = lax.ppermute(to_two, axes, by_core)
    back_one = lax.ppermute(to_one, "clu", opposite)
    incoming = jnp.concatenate(incoming, axis=0)
    incoming_other = swap(incoming, "rep")

    def forward_half(
        packed, incoming, incoming_other, matrix, near_row, near_col, row_held, col_held, block
    ):
        ahead, behind, full, held = forward_far(
            8,
            [
                (packed, lambda o, s, r: (2 * o,) * 2),
                (incoming, lambda o, s, r: (2 * (o ^ (1 + r)),) * 2 + (2 * (o ^ 3) + r - 2,)),
                (
                    incoming_other,
                    lambda o, s, r: (2 * (o ^ (2 - r)),) * 2 + (2 * (o ^ 3) + 1 - r - 2,),
                ),
            ],
            near_row,
            near_col,
            matrix,
            block,
        )
        own_rows = forward_own(row_held, col_held, held, full, width)
        payload, far = to_other_sub(ahead, swap(behind, "rep"), panels)
        return payload, far, own_rows

    payload, far, own_rows = stage(
        apart,
        forward_half,
        packed,
        incoming,
        incoming_other,
        matrix,
        near_row,
        near_col,
        row_held,
        col_held,
        near_block,
    )

    from_sub = swap(payload, "sub")
    backs = jnp.concatenate([back_two, back_one], axis=0)
    backs_other = swap(backs, "rep")
    own_other, own_rows_other = swap(own, "rep"), swap(own_rows, "rep")
    own_other, from_sub = lax.optimization_barrier((own_other, from_sub))
    from_sub_other = swap(from_sub.astype(jnp.float32), "rep")
    return finish(
        packed,
        (backs[:2], backs_other[:2]),
        ((own, backs[2:]), (own_other, backs_other[2:])),
        (own_rows, own_rows_other),
        (far,),
        (from_sub, from_sub_other),
    )


def shards_any(panel_field, near_row, near_col, near_block, bases, far_row, far_col, coupling):
    owner, sub, core = lax.axis_index("clu"), lax.axis_index("sub"), lax.axis_index("rep")
    owners, subs = lax.axis_size("clu"), lax.axis_size("sub")
    clusters, panels, width = panel_field.shape
    packed, _ = pack(panel_field, jnp.swapaxes(bases, 1, 2))
    around = lax.all_gather(packed, "sub", axis=0)
    gathered = lax.all_gather(packed, "clu", axis=0, tiled=True)
    slots = owners * clusters
    def slot_of(cluster, owner, core):
        return cluster

    held, matrix, _, _ = load(
        slots, near_row, near_col, far_row, far_col, coupling, near_block
    )
    back = back_sums(
        slots,
        slot_of,
        [(around[k], lambda o, s, r, k=k: (0, k)) for k in range(subs)],
        near_row,
        near_col,
        matrix,
        held,
    )
    back = lax.psum(lax.psum_scatter(back, "clu", scatter_dimension=0, tiled=True), "rep")
    ahead, behind, full, held = forward_far(
        slots, [(gathered, lambda o, s, r: (0,) * slots)], near_row, near_col, matrix, near_block
    )
    taken = swap(behind, "rep")
    near = forward_own(near_row, near_col, held, full, width)
    near = near + swap(near, "rep")
    far = lax.psum((ahead + taken)[(subs - 1) * panels :], "sub").reshape(clusters, -1, width)
    ahead = (ahead + taken)[: (subs - 1) * panels]
    for turn in range(1, subs):
        got = lax.ppermute(
            ahead[(turn - 1) * panels : turn * panels],
            "sub",
            [(s, (s + turn) % subs) for s in range(subs)],
        )
        near = near + jnp.where(core == 0, jnp.stack([got, swap(got, "rep")]), jnp.stack([swap(got, "rep"), got]))
    single = lax.dynamic_slice_in_dim(back, core, 1, axis=0)
    other = lax.dynamic_slice_in_dim(back, 1 - core, 1, axis=0)
    return finish(packed, (), ((single,), (other,)), (near,), (far,), ())


def shards(*arrays):
    sizes = tuple(lax.axis_size(axis) for axis in ("clu", "sub", "rep"))
    if sizes == (4, 2, 2):
        return shards_small(*arrays)
    return shards_any(*arrays)


def solution(mesh):
    placed = (
        P(("parts", "clu"), "sub", None),
        P(("parts", "clu", "rep")),
        P(("parts", "clu", "rep")),
        P(("parts", "clu", "rep"), None, "sub"),
        P(("parts", "clu"), "sub", None),
        P(("parts", "clu", "rep")),
        P(("parts", "clu", "rep")),
        P(("parts", "clu", "rep"), None, None),
    )
    return jax.shard_map(
        shards,
        mesh=mesh,
        in_specs=placed,
        out_specs=P(("parts", "clu"), "sub", None),
        check_vma=False,
    )
```
